32 devices in a mesh: case: 2 (over y), wall: 4 (over z), azim: 4 (over x, core).
Axes of the slice: x: 2, y: 2, z: 4, core: 2. Of those that a mesh axis runs over, the one named last changes fastest.
Arguments:
- state: float32 [12, 2, 32, 512], P(None, 'case', 'wall', 'azim'), parts along dimension 1, may hold values from 0.5 to 1.5
- courant: float32 [2, 32, 512], P('case', 'wall', 'azim'), parts along dimension 0, may hold values from -0.6 to 0.6
- cross_sections: float32 [64], replicated, may hold values from 0.02 to 0.6
- band_fractions: float32 [64], replicated, may hold values from 0.02 to 0.2
- absorb_index: int32 [11, 16], replicated, may hold values from 0 to 63
- band_index: int32 [16], replicated, may hold values from 0 to 63
Outputs:
- new_state: float32 [12, 2, 32, 512], P(None, 'case', 'wall', 'azim'), parts along dimension 1
- wall_flux: float32 [2, 512], P('case', 'azim'), parts along dimension 0
The draws below stay inside these ranges and needn't reach their ends.
There are 2 independent parts, one for each index of `case`. The reference program is written for one: setup_inputs(seed, part) draws one part's arguments, and reference() takes and returns one part's arrays. A program takes and returns all parts, laid end to end along the dimension named above; an argument that names none is the same for every part. Nothing has to cross between parts.
All inputs are finite; a program needn't handle non-finite values.
Results may differ from the reference program's by a relative error of at most 0.0003.
Values sent between devices are 32-bit elements; how exact they have to be, the bound alone decides.
No kernel may reach another device: no remote copies, remote signals or barrier semaphores. Data moves between devices by JAX's collectives and lax.ppermute only.
A program may use at most 64 MiB of HBM per device.

```python
import math
import jax
import jax.numpy as jnp
from jax import lax

STATIONS = 1
BANDS = 16
SPECIES = 11
NTAB = 64
COMPS = 12
NR = 32
NA = 512


def touch_ends(drawn, stream_key, low, largest):
    index_at = [jax.random.randint(jax.random.fold_in(stream_key, axis), (), 0, length) for axis, length in enumerate(drawn.shape)]
    main_axis = drawn.shape.index(max(drawn.shape))
    next_to = index_at[:main_axis] + [(index_at[main_axis] + 1) % drawn.shape[main_axis]] + index_at[main_axis + 1:]
    return drawn.at[tuple(index_at)].set(low).at[tuple(next_to)].set(largest)


def steps_of(stream_key, extent, pieces, least, high):
    factor_of, own = 1.0, jax.random.fold_in(stream_key, 6)
    for position, blocks in pieces:
        draws = jnp.exp(jax.random.uniform(jax.random.fold_in(own, position), (blocks,), jnp.float32, least / len(pieces), high / len(pieces)))
        factor_of = factor_of * jnp.repeat(draws, extent[position] // blocks).reshape([-1 if axis == position else 1 for axis in range(len(extent))])
    return factor_of


def setup_inputs(seed: int = 0, part: int = 0) -> dict:
    arg_keys = jax.random.split(jax.random.key(seed), 7)
    own_keys = jax.random.split(jax.random.fold_in(arg_keys[6], part), 7)
    return {
        "state": jnp.clip(0.5 + 1.0 * jax.random.uniform(own_keys[0], (COMPS, STATIONS, NR, NA), jnp.float32) ** steps_of(own_keys[0], (COMPS, STATIONS, NR, NA), ((2, 4), (3, 4)), -0.2, 0.2), 0.5, 1.5),
        "courant": jnp.clip(jax.random.uniform(own_keys[1], (STATIONS, NR, NA), jnp.float32, -0.6, 0.6) * steps_of(own_keys[1], (STATIONS, NR, NA), ((1, 4), (2, 4)), -0.4, 0.0), -0.6, 0.6),
        "cross_sections": jnp.clip(jnp.exp(jax.random.uniform(arg_keys[2], (NTAB,), jnp.float32, math.log(0.02), math.log(0.6))), 0.02, 0.6),
        "band_fractions": jnp.clip(jnp.exp(jax.random.uniform(arg_keys[3], (NTAB,), jnp.float32, math.log(0.02), math.log(0.2))), 0.02, 0.2),
        "absorb_index": touch_ends(jax.random.randint(arg_keys[4], (SPECIES, BANDS), 0, NTAB), jax.random.fold_in(arg_keys[4], 1), 0, NTAB - 1).astype(jnp.int32),
        "band_index": touch_ends(jax.random.randint(arg_keys[5], (BANDS,), 0, NTAB), jax.random.fold_in(arg_keys[5], 1), 0, NTAB - 1).astype(jnp.int32),
    }


KERNEL_WEIGHTS = (0.55, 0.45)
KERNEL_RATES = (1.15, 3.4)
FILTER_STRENGTH = 0.02
COUPLING = 0.1


def band_tables(absorb_index, band_index, cross_sections, band_fractions):
    entries = cross_sections.shape[0]
    table_slots = lax.broadcasted_iota(jnp.int32, (1, 1, entries), 2)
    spectral_absorber_area = jnp.sum(jnp.where(absorb_index[:, :, None] == table_slots, cross_sections[None, None, :], 0.0), axis=2)
    chosen_values = jnp.where(band_index[:, None] == table_slots[0], band_fractions[None, :], 0.0)
    return spectral_absorber_area, jnp.sum(chosen_values, axis=1)


def viewing_line_irradiance(kinetic_heat_level, species_concentrations, spectral_absorber_area, spectral_fraction_weight, mesh_cell_width, viewing_line_dimension):
    absorption = jnp.einsum("kb,kij->bij", spectral_absorber_area, species_concentrations, precision=lax.Precision.HIGHEST)
    optical_thickness_step = absorption * mesh_cell_width
    optical_depth = lax.cumsum(optical_thickness_step, viewing_line_dimension) - 0.5 * optical_thickness_step
    radiated_energy_rate = spectral_fraction_weight[:, None, None] * kinetic_heat_level[None] ** 4 * optical_thickness_step
    net_flux = 0.0
    wall_flux = 0.0
    for weight, decay_rate in zip(KERNEL_WEIGHTS, KERNEL_RATES):
        growth = jnp.exp(decay_rate * optical_depth)
        falloff = jnp.exp(-decay_rate * optical_depth)
        upward = falloff * lax.cumsum(radiated_energy_rate * growth, viewing_line_dimension)
        tail_sum = lax.cumsum(radiated_energy_rate * falloff, viewing_line_dimension, reverse=True)
        net_flux = net_flux + weight * jnp.sum(upward - growth * tail_sum, axis=0)
        wall_flux = wall_flux + weight * jnp.sum(lax.index_in_dim(tail_sum, 0, viewing_line_dimension, keepdims=False), axis=0)
    return net_flux, wall_flux


def edge_pad(net_flux, viewing_line_dimension):
    count = net_flux.shape[viewing_line_dimension]
    first_row = lax.slice_in_dim(net_flux, 0, 1, axis=viewing_line_dimension)
    last_row = lax.slice_in_dim(net_flux, count - 1, count, axis=viewing_line_dimension)
    return jnp.concatenate([first_row, net_flux, last_row], viewing_line_dimension)


def divergence(padded, viewing_line_dimension, mesh_cell_width):
    count = padded.shape[viewing_line_dimension] - 2
    before = lax.slice_in_dim(padded, 0, count, axis=viewing_line_dimension)
    after = lax.slice_in_dim(padded, 2, count + 2, axis=viewing_line_dimension)
    return (before - after) / (2.0 * mesh_cell_width)


def tendency(shifted, courant, heating):
    gradient = (45.0 * (shifted(1) - shifted(-1)) - 9.0 * (shifted(2) - shifted(-2)) + (shifted(3) - shifted(-3))) / 60.0
    smoothing = shifted(-3) + shifted(3) - 6.0 * (shifted(-2) + shifted(2)) + 15.0 * (shifted(-1) + shifted(1)) - 20.0 * shifted(0)
    change_sum = FILTER_STRENGTH * smoothing - courant[None] * gradient
    return change_sum.at[0].add(COUPLING * heating)


def reference(state, courant, cross_sections, band_fractions, absorb_index, band_index):
    spectral_absorber_area, spectral_fraction_weight = band_tables(absorb_index, band_index, cross_sections, band_fractions)
    mesh_cell_width = 1.0 / NR

    def segment_change(current):
        components = current.shape[0]
        line_data = jnp.transpose(current, (0, 2, 1, 3)).reshape(components, NR, STATIONS * NA)
        net_flux, wall_flux = viewing_line_irradiance(line_data[0], line_data[1:], spectral_absorber_area, spectral_fraction_weight, mesh_cell_width, 1)
        heating = divergence(edge_pad(net_flux, 0), 0, mesh_cell_width)
        heating = jnp.transpose(heating.reshape(NR, STATIONS, NA), (1, 0, 2))

        def shifted(offset):
            return jnp.roll(current, -offset, axis=3)

        return tendency(shifted, courant, heating), wall_flux.reshape(STATIONS, NA)

    first_change, first_flux = segment_change(state)
    middle = state + first_change
    second_change, second_flux = segment_change(middle)
    new_state = 0.5 * (state + middle + second_change)
    return new_state, 0.5 * (first_flux + second_flux)
```

```python
import functools

import jax
import jax.numpy as jnp
from jax import lax
from jax.experimental import pallas as pl
from jax.experimental.pallas import tpu as pltpu
from jax.sharding import PartitionSpec as P

KERNEL_WEIGHTS = (0.55, 0.45)
KERNEL_RATES = (1.15, 3.4)
COUPLING = 0.1
LOG2E = 1.4426950408889634
COMPS = 12
SPECIES = 11
BANDS = 16
EDGE = 6
COURANT = 12
TO_RIGHT = 13
TO_LEFT = 14
TILES = 15
HEAT_SLOT = 13
OFFSETS = (1, -1, 2, -2, 3, -3)


def lanes(shape):
    return lax.broadcasted_iota(jnp.int32, shape, len(shape) - 1)


def roll(x, shift):
    return pltpu.roll(x, shift % x.shape[-1], x.ndim - 1)


def pack_kernel(state_ref, courant_ref, block_ref):
    tile = courant_ref.shape
    cols = tile[-1]
    lane = lanes(tile)
    to_right = jnp.zeros(tile, jnp.float32)
    to_left = jnp.zeros(tile, jnp.float32)
    for k in range(COMPS + 1):
        value = state_ref[k] if k < COMPS else courant_ref[...]
        block_ref[k] = value
        here = (lane >= EDGE * k) & (lane < EDGE * (k + 1))
        to_right = jnp.where(here, roll(value, EDGE * k - (cols - EDGE)), to_right)
        to_left = jnp.where(here, roll(value, EDGE * k), to_left)
    block_ref[TO_RIGHT] = to_right
    block_ref[TO_LEFT] = to_left


def loop(count, body, carry):
    if count <= 4:
        for i in range(count):
            carry = body(i, carry)
        return carry
    return lax.fori_loop(0, count, body, carry)


def radiate(blocks, me, rows, cross_ref, share_ref, step_ref, emit_ref, decay_ref, up_ref, down_ref, net_ref, heat_ref):
    count = step_ref.shape[0]
    parts = count // rows
    cols = step_ref.shape[-1]

    def absorb(slot, carry):
        block = blocks(slot)
        base = (me ^ slot) * rows
        hot = block[0]
        hot = hot * hot
        hot = hot * hot
        for r in range(rows):
            step = None
            for k in range(SPECIES):
                term = cross_ref[k] * block[1 + k, pl.ds(r, 1), :]
                step = term if step is None else step + term
            step_ref[base + r] = step
            emit_ref[base + r] = share_ref[...] * step * hot[r : r + 1]
        return carry

    loop(parts, absorb, 0)

    def attenuate(part, before):
        for r in range(rows):
            at = part * rows + r
            step = step_ref[at]
            gap = before + step
            for i, rate in enumerate(KERNEL_RATES):
                decay_ref[i, at] = jnp.exp2(gap * (-0.5 * LOG2E * rate))
            before = step
        return before

    zero = jnp.zeros((BANDS, cols), jnp.float32)
    loop(parts, attenuate, zero)

    ratio = KERNEL_WEIGHTS[1] / KERNEL_WEIGHTS[0]

    def halve(x):
        return x[: BANDS // 2] + x[BANDS // 2 :]

    def sweep(part, carry):
        up0, up1, down0, down1 = carry
        for r in range(rows):
            at = part * rows + r
            emitted = emit_ref[at]
            up0 = up0 * decay_ref[0, at] + emitted
            up1 = up1 * decay_ref[1, at] + emitted
            up_ref[at] = halve(up0 + ratio * up1)
            back = count - 1 - at
            emitted = emit_ref[back]
            down0 = down0 + emitted
            down1 = down1 + emitted
            down_ref[back] = halve(down0 + ratio * down1)
            down0 = down0 * decay_ref[0, back]
            down1 = down1 * decay_ref[1, back]
        return up0, up1, down0, down1

    _, _, down0, down1 = loop(parts, sweep, (zero, zero, zero, zero))
    wall = KERNEL_WEIGHTS[0] * jnp.sum(down0 + ratio * down1, axis=0, keepdims=True)

    def combine(part, carry):
        rows_here = pl.ds(part * rows, rows)
        net = jnp.sum(up_ref[rows_here] - down_ref[rows_here], axis=1)
        net_ref[pl.ds(pl.multiple_of(part * rows + rows, rows), rows), :] = net
        return carry

    loop(parts, combine, 0)
    net_ref[rows - 1 : rows, :] = net_ref[rows : rows + 1, :]
    net_ref[rows + count : rows + count + 1, :] = net_ref[rows + count - 1 : rows + count, :]
    scale = KERNEL_WEIGHTS[0] * count / 2.0
    for part in range(parts):
        first = part * rows + rows
        heat_ref[part] = (net_ref[first - 1 : first - 1 + rows, :] - net_ref[first + 1 : first + 1 + rows, :]) * scale
    return wall


def slot_of(slots, s):
    return slots[0].at[s] if len(slots) == 1 else slots[s]


def first_kernel(given, parts, *refs):
    slots = refs[:given]
    cross_ref, share_ref, heating_ref, wall_ref, right_ref, left_ref = refs[given : given + 6]
    scratch = refs[given + 6 :]
    heat_ref = scratch[-1]
    tile = heating_ref.shape[1:]
    rows, cols = tile
    me = lax.axis_index("wall")
    wall_ref[...] = radiate(lambda s: slot_of(slots, s), me, rows, cross_ref, share_ref, *scratch)
    for s in range(parts):
        heating = heat_ref[me ^ s]
        heating_ref[s] = heating
        block = slot_of(slots, s)
        to_right = block[TO_RIGHT]
        to_left = block[TO_LEFT]
        if s == 0:
            lane = lanes(tile)
            here = (lane >= EDGE * HEAT_SLOT) & (lane < EDGE * (HEAT_SLOT + 1))
            to_right = jnp.where(here, roll(heating, EDGE * HEAT_SLOT - (cols - EDGE)), to_right)
            to_left = jnp.where(here, roll(heating, EDGE * HEAT_SLOT), to_left)
        right_ref[s] = to_right
        left_ref[s] = to_left


def coefficients(courant):
    return (0.3 - 0.75 * courant, 0.3 + 0.75 * courant, 0.15 * courant - 0.12, -0.12 - 0.15 * courant, 0.02 - courant / 60.0, 0.02 + courant / 60.0)


def stencil(value, halo, factors, lane, cols):
    total = 0.6 * value
    for offset, factor in zip(OFFSETS, factors):
        if halo is None:
            source = value
        elif offset > 0:
            source = jnp.where(lane < offset, halo, value)
        else:
            source = jnp.where(lane >= cols + offset, halo, value)
        total = total + factor * roll(source, -offset)
    return total


def second_kernel(given, parts, *refs):
    slots = refs[:given]
    (heating_ref, wall_in_ref, from_left_ref, from_right_ref, cross_ref, share_ref, out_ref, wall_ref, middle_ref, edge_ref) = refs[given : given + 10]
    scratch = refs[given + 10 :]
    own = slot_of(slots, 0)
    heat_ref = scratch[-1]
    tile = heating_ref.shape[1:]
    rows, cols = tile
    half = cols // 2
    lane = lanes(tile)
    me = lax.axis_index("wall")

    def advance(s, carry):
        left, right = from_left_ref[s], from_right_ref[s]
        three = EDGE // 2
        both = jnp.where(lane % EDGE < three, roll(left, -three), roll(right, three))
        block = slot_of(slots, s)
        factors = coefficients(block[COURANT])
        for k in range(COMPS):
            halo = roll(both, -(EDGE * k + three))
            moved = stencil(block[k], halo, factors, lane, cols)
            if k == 0:
                moved = moved + COUPLING * heating_ref[s]
            middle_ref[s, k] = moved
        return carry

    loop(parts, advance, 0)

    left, right = from_left_ref[0], from_right_ref[0]

    def placed(k, value):
        from_left = roll(left, half - EDGE - EDGE * k)
        from_right = roll(right, -EDGE * k)
        inner = from_left
        if value is not None:
            inner = jnp.where(lane < half, from_left, jnp.where(lane < half + half // 2, roll(value, half), value))
        return jnp.where(lane < EDGE, from_right, inner)

    factors = coefficients(placed(COURANT, None))
    for k in range(COMPS):
        moved = stencil(placed(k, own[k]), None, factors, lane, cols)
        if k == 0:
            moved = moved + COUPLING * placed(HEAT_SLOT, None)
        edge_ref[k] = jnp.where(lane < half // 2, moved, roll(moved, half))

    wall = radiate(lambda s: middle_ref.at[s], me, rows, cross_ref, share_ref, *scratch)
    wall_ref[...] = 0.5 * (wall_in_ref[...] + wall)
    heating = heat_ref[me]
    factors = coefficients(own[COURANT])
    for k in range(COMPS):
        moved = stencil(middle_ref[0, k], edge_ref[k], factors, lane, cols)
        if k == 0:
            moved = moved + COUPLING * heating
        out_ref[k] = 0.5 * (own[k] + moved)


def band_tables(absorb_index, band_index, cross_sections, band_fractions, height, cols):
    entries = cross_sections.shape[0]
    table_slots = lax.broadcasted_iota(jnp.int32, (1, 1, entries), 2)
    area = jnp.sum(jnp.where(absorb_index[:, :, None] == table_slots, cross_sections[None, None, :], 0.0), axis=2)
    share = jnp.sum(jnp.where(band_index[:, None] == table_slots[0], band_fractions[None, :], 0.0), axis=1)
    area = jnp.broadcast_to((area * height)[:, :, None], area.shape + (cols,))
    return area, jnp.broadcast_to(share[:, None], share.shape + (cols,))


def exchange(x, axis, distance):
    return lax.ppermute(x, axis, [(i, i ^ distance) for i in range(lax.axis_size(axis))])


def gather_lines(block, axis):
    count = lax.axis_size(axis)
    distance = count // 2
    if count > 4:
        stack = block[None]
        for step in range(count.bit_length() - 1):
            stack = jnp.concatenate([stack, exchange(stack, axis, 1 << step)])
        return [stack]
    held = {0: block}
    while distance:
        for slot in list(held):
            held[slot ^ distance] = exchange(held[slot], axis, distance)
        distance //= 2
    return [held[s] for s in range(count)]


def call(kernel, outs, scratch, *args):
    vmem = pl.BlockSpec(memory_space=pltpu.VMEM)
    return pl.pallas_call(
        kernel,
        out_shape=[jax.ShapeDtypeStruct(shape, jnp.float32) for shape in outs],
        in_specs=[vmem] * len(args),
        out_specs=[vmem] * len(outs),
        scratch_shapes=[pltpu.VMEM(shape, jnp.float32) for shape in scratch],
        compiler_params=pltpu.CompilerParams(vmem_limit_bytes=32 * 1024 * 1024),
    )(*args)


def local(state, courant, cross_sections, band_fractions, absorb_index, band_index):
    comps, stations, rows, cols = state.shape
    parts = lax.axis_size("wall")
    count = parts * rows
    ring = lax.axis_size("azim")
    tile = (rows, cols)
    (block,) = call(pack_kernel, [(TILES,) + tile], [], state.reshape(comps, rows, cols), courant.reshape(tile))
    slots = gather_lines(block, "wall")
    cross, share = band_tables(absorb_index, band_index, cross_sections, band_fractions, 1.0 / count, cols)
    deep = (count, BANDS, cols)
    flat = (count, BANDS // 2, cols)
    scratch = [deep, deep, (2,) + deep, flat, flat, (count + 2 * rows, cols), (parts,) + tile]
    whole = (parts,) + tile
    heating, wall, right, left = call(
        functools.partial(first_kernel, len(slots), parts), [whole, (1, cols), whole, whole], scratch, *slots, cross, share
    )
    from_left = lax.ppermute(right, "azim", [(i, (i + 1) % ring) for i in range(ring)])
    from_right = lax.ppermute(left, "azim", [(i, (i - 1) % ring) for i in range(ring)])
    middle = (parts, comps) + tile
    new_state, wall = call(
        functools.partial(second_kernel, len(slots), parts),
        [(comps,) + tile, (1, cols)],
        [middle, (comps,) + tile] + scratch,
        *slots, heating, wall, from_left, from_right, cross, share,
    )
    return new_state.reshape(state.shape), wall


def solution(mesh):
    return jax.shard_map(
        local,
        mesh=mesh,
        in_specs=(P(None, "case", "wall", "azim"), P("case", "wall", "azim"), P(), P(), P(), P()),
        out_specs=(P(None, "case", "wall", "azim"), P("case", "azim")),
        check_vma=False,
    )
```

```python
import functools

import jax
import jax.numpy as jnp
from jax import lax
from jax.experimental import pallas as pl
from jax.experimental.pallas import tpu as pltpu
from jax.sharding import PartitionSpec as P

KERNEL_WEIGHTS = (0.55, 0.45)
KERNEL_RATES = (1.15, 3.4)
COUPLING = 0.1
LOG2E = 1.4426950408889634
COMPS = 12
SPECIES = 11
BANDS = 16
EDGE = 6
COURANT = 12
TO_RIGHT = 13
TO_LEFT = 14
TILES = 15
HEAT_SLOT = 13
OFFSETS = (1, -1, 2, -2, 3, -3)


def lanes(shape):
    return lax.broadcasted_iota(jnp.int32, shape, len(shape) - 1)


def roll(x, shift):
    return pltpu.roll(x, shift % x.shape[-1], x.ndim - 1)


def pack_kernel(state_ref, courant_ref, block_ref):
    tile = courant_ref.shape
    cols = tile[-1]
    lane = lanes(tile)
    to_right = jnp.zeros(tile, jnp.float32)
    to_left = jnp.zeros(tile, jnp.float32)
    for k in range(COMPS + 1):
        value = state_ref[k] if k < COMPS else courant_ref[...]
        block_ref[k] = value
        here = (lane >= EDGE * k) & (lane < EDGE * (k + 1))
        to_right = jnp.where(here, roll(value, EDGE * k - (cols - EDGE)), to_right)
        to_left = jnp.where(here, roll(value, EDGE * k), to_left)
    block_ref[TO_RIGHT] = to_right
    block_ref[TO_LEFT] = to_left


def loop(count, body, carry):
    if count <= 4:
        for i in range(count):
            carry = body(i, carry)
        return carry
    return lax.fori_loop(0, count, body, carry)


def radiate(blocks, me, rows, cross_ref, share_ref, step_ref, emit_ref, decay_ref, up_ref, down_ref, net_ref, heat_ref):
    count = step_ref.shape[0]
    parts = count // rows
    cols = step_ref.shape[-1]

    def absorb(slot, carry):
        block = blocks(slot)
        base = (me ^ slot) * rows
        hot = block[0]
        hot = hot * hot
        hot = hot * hot
        for r in range(rows):
            step = None
            for k in range(SPECIES):
                term = cross_ref[k] * block[1 + k, pl.ds(r, 1), :]
                step = term if step is None else step + term
            step_ref[base + r] = step
            emit_ref[base + r] = share_ref[...] * step * hot[r : r + 1]
        return carry

    loop(parts, absorb, 0)

    def attenuate(part, before):
        for r in range(rows):
            at = part * rows + r
            step = step_ref[at]
            gap = before + step
            for i, rate in enumerate(KERNEL_RATES):
                decay_ref[i, at] = jnp.exp2(gap * (-0.5 * LOG2E * rate))
            before = step
        return before

    zero = jnp.zeros((BANDS, cols), jnp.float32)
    loop(parts, attenuate, zero)

    ratio = KERNEL_WEIGHTS[1] / KERNEL_WEIGHTS[0]

    def halve(x):
        return x[: BANDS // 2] + x[BANDS // 2 :]

    def sweep(part, carry):
        up0, up1, down0, down1 = carry
        for r in range(rows):
            at = part * rows + r
            emitted = emit_ref[at]
            up0 = up0 * decay_ref[0, at] + emitted
            up1 = up1 * decay_ref[1, at] + emitted
            up_ref[at] = halve(up0 + ratio * up1)
            back = count - 1 - at
            emitted = emit_ref[back]
            down0 = down0 + emitted
            down1 = down1 + emitted
            down_ref[back] = halve(down0 + ratio * down1)
            down0 = down0 * decay_ref[0, back]
            down1 = down1 * decay_ref[1, back]
        return up0, up1, down0, down1

    _, _, down0, down1 = loop(parts, sweep, (zero, zero, zero, zero))
    wall = KERNEL_WEIGHTS[0] * jnp.sum(down0 + ratio * down1, axis=0, keepdims=True)

    def combine(part, carry):
        rows_here = pl.ds(part * rows, rows)
        net = jnp.sum(up_ref[rows_here] - down_ref[rows_here], axis=1)
        net_ref[pl.ds(pl.multiple_of(part * rows + rows, rows), rows), :] = net
        return carry

    loop(parts, combine, 0)
    net_ref[rows - 1 : rows, :] = net_ref[rows : rows + 1, :]
    net_ref[rows + count : rows + count + 1, :] = net_ref[rows + count - 1 : rows + count, :]
    scale = KERNEL_WEIGHTS[0] * count / 2.0
    for part in range(parts):
        first = part * rows + rows
        heat_ref[part] = (net_ref[first - 1 : first - 1 + rows, :] - net_ref[first + 1 : first + 1 + rows, :]) * scale
    return wall


def slot_of(slots, s):
    return slots[0].at[s] if len(slots) == 1 else slots[s]


def first_kernel(given, parts, *refs):
    slots = refs[:given]
    cross_ref, share_ref, heating_ref, wall_ref, right_ref, left_ref = refs[given : given + 6]
    scratch = refs[given + 6 :]
    heat_ref = scratch[-1]
    tile = heating_ref.shape[1:]
    rows, cols = tile
    me = lax.axis_index("wall")
    wall_ref[...] = radiate(lambda s: slot_of(slots, s), me, rows, cross_ref, share_ref, *scratch)
    for s in range(parts):
        heating = heat_ref[me ^ s]
        heating_ref[s] = heating
        block = slot_of(slots, s)
        to_right = block[TO_RIGHT]
        to_left = block[TO_LEFT]
        if s == 0:
            lane = lanes(tile)
            here = (lane >= EDGE * HEAT_SLOT) & (lane < EDGE * (HEAT_SLOT + 1))
            to_right = jnp.where(here, roll(heating, EDGE * HEAT_SLOT - (cols - EDGE)), to_right)
            to_left = jnp.where(here, roll(heating, EDGE * HEAT_SLOT), to_left)
        right_ref[s] = to_right
        left_ref[s] = to_left


def coefficients(courant):
    return (0.3 - 0.75 * courant, 0.3 + 0.75 * courant, 0.15 * courant - 0.12, -0.12 - 0.15 * courant, 0.02 - courant / 60.0, 0.02 + courant / 60.0)


def stencil(value, halo, factors, lane, cols):
    total = 0.6 * value
    for offset, factor in zip(OFFSETS, factors):
        if halo is None:
            source = value
        elif offset > 0:
            source = jnp.where(lane < offset, halo, value)
        else:
            source = jnp.where(lane >= cols + offset, halo, value)
        total = total + factor * roll(source, -offset)
    return total


def advance_kernel(given, parts, *refs):
    slots = refs[:given]
    heating_ref, from_left_ref, from_right_ref, middle_ref, edge_ref, halo_ref, near_ref = refs[given:]
    own = slot_of(slots, 0)
    tile = heating_ref.shape[1:]
    rows, cols = tile
    half = cols // 2
    lane = lanes(tile)
    three = EDGE // 2
    first_half = lax.rem(lane, EDGE) < three

    def place(s, carry):
        both = jnp.where(first_half, roll(from_left_ref[s], -three), roll(from_right_ref[s], three))
        for k in range(COMPS):
            halo_ref[s, k] = roll(both, -(EDGE * k + three))
        return carry

    loop(parts, place, 0)

    left, right = from_left_ref[0], from_right_ref[0]
    for k in range(HEAT_SLOT + 1):
        from_left = roll(left, half - EDGE - EDGE * k)
        from_right = roll(right, -EDGE * k)
        inner = from_left
        if k < COMPS:
            value = own[k]
            inner = jnp.where(lane < half, from_left, jnp.where(lane < half + half // 2, roll(value, half), value))
        near_ref[k] = jnp.where(lane < EDGE, from_right, inner)

    def advance(s, carry):
        block = slot_of(slots, s)
        factors = coefficients(block[COURANT])
        for k in range(COMPS):
            moved = stencil(block[k], halo_ref[s, k], factors, lane, cols)
            if k == 0:
                moved = moved + COUPLING * heating_ref[s]
            middle_ref[s, k] = moved
        return carry

    loop(parts, advance, 0)

    factors = coefficients(near_ref[COURANT])
    for k in range(COMPS):
        moved = stencil(near_ref[k], None, factors, lane, cols)
        if k == 0:
            moved = moved + COUPLING * near_ref[HEAT_SLOT]
        halo_ref[0, k] = moved
    for k in range(COMPS):
        moved = halo_ref[0, k]
        edge_ref[k] = jnp.where(lane < half // 2, moved, roll(moved, half))


def last_kernel(given, block_ref, middle_ref, edge_ref, wall_in_ref, cross_ref, share_ref, out_ref, wall_ref, *scratch):
    heat_ref = scratch[-1]
    own = block_ref if given > 1 else block_ref.at[0]
    rows, cols = out_ref.shape[1:]
    lane = lanes((rows, cols))
    me = lax.axis_index("wall")
    wall = radiate(lambda s: middle_ref.at[s], me, rows, cross_ref, share_ref, *scratch)
    wall_ref[...] = 0.5 * (wall_in_ref[...] + wall)
    factors = coefficients(own[COURANT])
    for k in range(COMPS):
        moved = stencil(middle_ref[0, k], edge_ref[k], factors, lane, cols)
        if k == 0:
            moved = moved + COUPLING * heat_ref[me]
        out_ref[k] = 0.5 * (own[k] + moved)


def band_tables(absorb_index, band_index, cross_sections, band_fractions, height, cols):
    entries = cross_sections.shape[0]
    table_slots = lax.broadcasted_iota(jnp.int32, (1, 1, entries), 2)
    area = jnp.sum(jnp.where(absorb_index[:, :, None] == table_slots, cross_sections[None, None, :], 0.0), axis=2)
    share = jnp.sum(jnp.where(band_index[:, None] == table_slots[0], band_fractions[None, :], 0.0), axis=1)
    area = jnp.broadcast_to((area * height)[:, :, None], area.shape + (cols,))
    return area, jnp.broadcast_to(share[:, None], share.shape + (cols,))


def exchange(x, axis, distance):
    return lax.ppermute(x, axis, [(i, i ^ distance) for i in range(lax.axis_size(axis))])


def gather_lines(block, axis):
    count = lax.axis_size(axis)
    distance = count // 2
    if count > 4:
        stack = block[None]
        for step in range(count.bit_length() - 1):
            stack = jnp.concatenate([stack, exchange(stack, axis, 1 << step)])
        return [stack]
    held = {0: block}
    while distance:
        for slot in list(held):
            held[slot ^ distance] = exchange(held[slot], axis, distance)
        distance //= 2
    return [held[s] for s in range(count)]


def call(kernel, outs, scratch, *args):
    vmem = pl.BlockSpec(memory_space=pltpu.VMEM)
    return pl.pallas_call(
        kernel,
        out_shape=[jax.ShapeDtypeStruct(shape, jnp.float32) for shape in outs],
        in_specs=[vmem] * len(args),
        out_specs=[vmem] * len(outs),
        scratch_shapes=[pltpu.VMEM(shape, jnp.float32) for shape in scratch],
        compiler_params=pltpu.CompilerParams(vmem_limit_bytes=32 * 1024 * 1024),
    )(*args)


def local(state, courant, cross_sections, band_fractions, absorb_index, band_index):
    comps, stations, rows, cols = state.shape
    parts = lax.axis_size("wall")
    count = parts * rows
    ring = lax.axis_size("azim")
    tile = (rows, cols)
    (block,) = call(pack_kernel, [(TILES,) + tile], [], state.reshape(comps, rows, cols), courant.reshape(tile))
    slots = gather_lines(block, "wall")
    cross, share = band_tables(absorb_index, band_index, cross_sections, band_fractions, 1.0 / count, cols)
    deep = (count, BANDS, cols)
    flat = (count, BANDS // 2, cols)
    scratch = [deep, deep, (2,) + deep, flat, flat, (count + 2 * rows, cols), (parts,) + tile]
    whole = (parts,) + tile
    heating, wall, right, left = call(
        functools.partial(first_kernel, len(slots), parts), [whole, (1, cols), whole, whole], scratch, *slots, cross, share
    )
    from_left = lax.ppermute(right, "azim", [(i, (i + 1) % ring) for i in range(ring)])
    from_right = lax.ppermute(left, "azim", [(i, (i - 1) % ring) for i in range(ring)])
    middle, edge = call(
        functools.partial(advance_kernel, len(slots), parts),
        [(parts, comps) + tile, (comps,) + tile],
        [(parts, comps) + tile, (HEAT_SLOT + 1,) + tile],
        *slots, heating, from_left, from_right,
    )
    new_state, wall = call(
        functools.partial(last_kernel, len(slots)), [(comps,) + tile, (1, cols)], scratch,
        slots[0], middle, edge, wall, cross, share,
    )
    return new_state.reshape(state.shape), wall


def solution(mesh):
    return jax.shard_map(
        local,
        mesh=mesh,
        in_specs=(P(None, "case", "wall", "azim"), P("case", "wall", "azim"), P(), P(), P(), P()),
        out_specs=(P(None, "case", "wall", "azim"), P("case", "azim")),
        check_vma=False,
    )
```

```python
import functools

import jax
import jax.numpy as jnp
from jax import lax
from jax.experimental import pallas as pl
from jax.experimental.pallas import tpu as pltpu
from jax.sharding import PartitionSpec as P

KERNEL_WEIGHTS = (0.55, 0.45)
KERNEL_RATES = (1.15, 3.4)
COUPLING = 0.1
LOG2E = 1.4426950408889634
COMPS = 12
SPECIES = 11
BANDS = 16
EDGE = 6
COURANT = 12
TILES = 13
HEAT_SLOT = 13
OFFSETS = (1, -1, 2, -2, 3, -3)


def lanes(shape):
    return lax.broadcasted_iota(jnp.int32, shape, len(shape) - 1)


def roll(x, shift):
    return pltpu.roll(x, shift % x.shape[-1], x.ndim - 1)


def pack_kernel(state_ref, courant_ref, block_ref, sems):
    copies = [
        pltpu.make_async_copy(state_ref, block_ref.at[pl.ds(0, COMPS)], sems.at[0]),
        pltpu.make_async_copy(courant_ref, block_ref.at[COURANT], sems.at[1]),
    ]
    for copy in copies:
        copy.start()
    for copy in copies:
        copy.wait()


def edge_tiles(block, lane, extra):
    cols = lane.shape[-1]
    last = jnp.zeros(lane.shape, jnp.float32)
    first = jnp.zeros(lane.shape, jnp.float32)
    for k in range(COMPS + 2):
        if k <= COMPS:
            value = block[k]
        elif extra is not None:
            value = extra
        else:
            continue
        here = (lane >= EDGE * k) & (lane < EDGE * (k + 1))
        last = jnp.where(here, roll(value, EDGE * k - (cols - EDGE)), last)
        first = jnp.where(here, roll(value, EDGE * k), first)
    return last, first


def loop(count, body, carry):
    if count <= 4:
        for i in range(count):
            carry = body(i, carry)
        return carry
    return lax.fori_loop(0, count, body, carry)


def radiate(blocks, me, rows, cross_ref, share_ref, step_ref, emit_ref, decay_ref, up_ref, down_ref, net_ref, heat_ref):
    count = step_ref.shape[0]
    parts = count // rows
    cols = step_ref.shape[-1]

    def absorb(slot, carry):
        block = blocks(slot)
        base = (me ^ slot) * rows
        hot = block[0]
        hot = hot * hot
        hot = hot * hot
        for r in range(rows):
            step = None
            for k in range(SPECIES):
                term = cross_ref[k] * block[1 + k, pl.ds(r, 1), :]
                step = term if step is None else step + term
            step_ref[base + r] = step
            emit_ref[base + r] = share_ref[...] * step * hot[r : r + 1]
        return carry

    loop(parts, absorb, 0)

    def attenuate(part, before):
        for r in range(rows):
            at = part * rows + r
            step = step_ref[at]
            gap = before + step
            for i, rate in enumerate(KERNEL_RATES):
                decay_ref[i, at] = jnp.exp2(gap * (-0.5 * LOG2E * rate))
            before = step
        return before

    zero = jnp.zeros((BANDS, cols), jnp.float32)
    loop(parts, attenuate, zero)

    ratio = KERNEL_WEIGHTS[1] / KERNEL_WEIGHTS[0]

    def halve(x):
        return x[: BANDS // 2] + x[BANDS // 2 :]

    def sweep(part, carry):
        up0, up1, down0, down1 = carry
        for r in range(rows):
            at = part * rows + r
            emitted = emit_ref[at]
            up0 = up0 * decay_ref[0, at] + emitted
            up1 = up1 * decay_ref[1, at] + emitted
            up_ref[at] = halve(up0 + ratio * up1)
            back = count - 1 - at
            emitted = emit_ref[back]
            down0 = down0 + emitted
            down1 = down1 + emitted
            down_ref[back] = halve(down0 + ratio * down1)
            down0 = down0 * decay_ref[0, back]
            down1 = down1 * decay_ref[1, back]
        return up0, up1, down0, down1

    _, _, down0, down1 = loop(parts, sweep, (zero, zero, zero, zero))
    wall = KERNEL_WEIGHTS[0] * jnp.sum(down0 + ratio * down1, axis=0, keepdims=True)

    def combine(part, carry):
        rows_here = pl.ds(part * rows, rows)
        net = jnp.sum(up_ref[rows_here] - down_ref[rows_here], axis=1)
        net_ref[pl.ds(pl.multiple_of(part * rows + rows, rows), rows), :] = net
        return carry

    loop(parts, combine, 0)
    net_ref[rows - 1 : rows, :] = net_ref[rows : rows + 1, :]
    net_ref[rows + count : rows + count + 1, :] = net_ref[rows + count - 1 : rows + count, :]
    scale = KERNEL_WEIGHTS[0] * count / 2.0
    for part in range(parts):
        first = part * rows + rows
        heat_ref[part] = (net_ref[first - 1 : first - 1 + rows, :] - net_ref[first + 1 : first + 1 + rows, :]) * scale
    return wall


def slot_of(slots, s):
    return slots[0].at[s] if len(slots) == 1 else slots[s]


def first_kernel(given, parts, *refs):
    slots = refs[:given]
    cross_ref, share_ref, heating_ref, wall_ref, outer_ref, inner_ref = refs[given : given + 6]
    scratch = refs[given + 6 :]
    heat_ref = scratch[-1]
    tile = heating_ref.shape[1:]
    rows, cols = tile
    me = lax.axis_index("wall")
    wall_ref[...] = radiate(lambda s: slot_of(slots, s), me, rows, cross_ref, share_ref, *scratch)
    lane = lanes(tile)
    odd = lax.rem(lax.axis_index("azim"), 2) == 1
    for s in range(parts):
        heating = heat_ref[me ^ s]
        heating_ref[s] = heating
        last, first = edge_tiles(slot_of(slots, s), lane, heating if s == 0 else None)
        outer_ref[s] = jnp.where(odd, last, first)
        inner_ref[s] = jnp.where(odd, first, last)


def coefficients(courant):
    return (0.3 - 0.75 * courant, 0.3 + 0.75 * courant, 0.15 * courant - 0.12, -0.12 - 0.15 * courant, 0.02 - courant / 60.0, 0.02 + courant / 60.0)


def stencil(value, halo, factors, lane, cols):
    total = 0.6 * value
    for offset, factor in zip(OFFSETS, factors):
        if halo is None:
            source = value
        elif offset > 0:
            source = jnp.where(lane < offset, halo, value)
        else:
            source = jnp.where(lane >= cols + offset, halo, value)
        total = total + factor * roll(source, -offset)
    return total


def advance_kernel(given, parts, *refs):
    slots = refs[:given]
    heating_ref, outer_ref, inner_ref, middle_ref, edge_ref, halo_ref, near_ref = refs[given:]
    own = slot_of(slots, 0)
    tile = heating_ref.shape[1:]
    rows, cols = tile
    half = cols // 2
    lane = lanes(tile)
    three = EDGE // 2
    first_half = lax.rem(lane, EDGE) < three
    odd = lax.rem(lax.axis_index("azim"), 2) == 1

    def received(s):
        outer, inner = outer_ref[s], inner_ref[s]
        return jnp.where(odd, inner, outer), jnp.where(odd, outer, inner)

    def place(s, carry):
        left, right = received(s)
        both = jnp.where(first_half, roll(left, -three), roll(right, three))
        for k in range(COMPS):
            halo_ref[s, k] = roll(both, -(EDGE * k + three))
        return carry

    loop(parts, place, 0)

    left, right = received(0)
    for k in range(HEAT_SLOT + 1):
        from_left = roll(left, half - EDGE - EDGE * k)
        from_right = roll(right, -EDGE * k)
        inner = from_left
        if k < COMPS:
            value = own[k]
            inner = jnp.where(lane < half, from_left, jnp.where(lane < half + half // 2, roll(value, half), value))
        near_ref[k] = jnp.where(lane < EDGE, from_right, inner)

    def advance(s, carry):
        block = slot_of(slots, s)
        factors = coefficients(block[COURANT])
        for k in range(COMPS):
            moved = stencil(block[k], halo_ref[s, k], factors, lane, cols)
            if k == 0:
                moved = moved + COUPLING * heating_ref[s]
            middle_ref[s, k] = moved
        return carry

    loop(parts, advance, 0)

    factors = coefficients(near_ref[COURANT])
    for k in range(COMPS):
        moved = stencil(near_ref[k], None, factors, lane, cols)
        if k == 0:
            moved = moved + COUPLING * near_ref[HEAT_SLOT]
        halo_ref[0, k] = moved
    for k in range(COMPS):
        moved = halo_ref[0, k]
        edge_ref[k] = jnp.where(lane < half // 2, moved, roll(moved, half))


def last_kernel(given, block_ref, middle_ref, edge_ref, wall_in_ref, cross_ref, share_ref, out_ref, wall_ref, *scratch):
    heat_ref = scratch[-1]
    own = block_ref if given > 1 else block_ref.at[0]
    rows, cols = out_ref.shape[1:]
    lane = lanes((rows, cols))
    me = lax.axis_index("wall")
    wall = radiate(lambda s: middle_ref.at[s], me, rows, cross_ref, share_ref, *scratch)
    wall_ref[...] = 0.5 * (wall_in_ref[...] + wall)
    factors = coefficients(own[COURANT])
    for k in range(COMPS):
        moved = stencil(middle_ref[0, k], edge_ref[k], factors, lane, cols)
        if k == 0:
            moved = moved + COUPLING * heat_ref[me]
        out_ref[k] = 0.5 * (own[k] + moved)


def band_tables(absorb_index, band_index, cross_sections, band_fractions, height, cols):
    entries = cross_sections.shape[0]
    table_slots = lax.broadcasted_iota(jnp.int32, (1, 1, entries), 2)
    area = jnp.sum(jnp.where(absorb_index[:, :, None] == table_slots, cross_sections[None, None, :], 0.0), axis=2)
    share = jnp.sum(jnp.where(band_index[:, None] == table_slots[0], band_fractions[None, :], 0.0), axis=1)
    area = jnp.broadcast_to((area * height)[:, :, None], area.shape + (cols,))
    return area, jnp.broadcast_to(share[:, None], share.shape + (cols,))


def exchange(x, axis, distance):
    return lax.ppermute(x, axis, [(i, i ^ distance) for i in range(lax.axis_size(axis))])


def gather_lines(block, axis, tables):
    count = lax.axis_size(axis)
    distance = count // 2
    if count > 4:
        stack = block[None]
        for step in range(count.bit_length() - 1):
            stack = jnp.concatenate([stack, exchange(stack, axis, 1 << step)])
        return [stack], tables
    held = {0: block}
    for d in (3,2,1): held[d]=exchange(block,axis,d)
    return [held[s] for s in range(count)], tables


VMEM = pl.BlockSpec(memory_space=pltpu.VMEM)


def call(kernel, outs, scratch, *args, in_specs=None, limit=32 * 1024 * 1024):
    return pl.pallas_call(
        kernel,
        out_shape=[jax.ShapeDtypeStruct(shape, jnp.float32) for shape in outs],
        in_specs=in_specs or [VMEM] * len(args),
        out_specs=[VMEM] * len(outs),
        scratch_shapes=[pltpu.VMEM(shape, jnp.float32) if isinstance(shape, tuple) else shape for shape in scratch],
        compiler_params=pltpu.CompilerParams(vmem_limit_bytes=limit),
    )(*args)


def local(state, courant, cross_sections, band_fractions, absorb_index, band_index):
    comps, stations, rows, cols = state.shape
    parts = lax.axis_size("wall")
    count = parts * rows
    ring = lax.axis_size("azim")
    tile = (rows, cols)
    block = jnp.concatenate([state.reshape(comps, rows, cols), courant.reshape((1,) + tile)])
    tables = band_tables(absorb_index, band_index, cross_sections, band_fractions, 1.0 / count, cols)
    slots, (cross, share) = gather_lines(block, "wall", tables)
    deep = (count, BANDS, cols)
    flat = (count, BANDS // 2, cols)
    scratch = [deep, deep, (2,) + deep, flat, flat, (count + 2 * rows, cols), (parts,) + tile]
    whole = (parts,) + tile
    heating, wall, outer, inner = call(
        functools.partial(first_kernel, len(slots), parts), [whole, (1, cols), whole, whole], scratch, *slots, cross, share
    )
    inner = lax.ppermute(inner, "azim", [(i, i ^ 1) for i in range(ring)])
    outer = lax.ppermute(outer, "azim", [(i, (i + 1) % ring if i % 2 else (i - 1) % ring) for i in range(ring)])
    middle, edge = call(
        functools.partial(advance_kernel, len(slots), parts),
        [(parts, comps) + tile, (comps,) + tile],
        [(parts, comps) + tile, (HEAT_SLOT + 1,) + tile],
        *slots, heating, outer, inner,
    )
    new_state, wall = call(
        functools.partial(last_kernel, len(slots)), [(comps,) + tile, (1, cols)], scratch,
        slots[0], middle, edge, wall, cross, share,
    )
    return new_state.reshape(state.shape), wall


def solution(mesh):
    return jax.shard_map(
        local,
        mesh=mesh,
        in_specs=(P(None, "case", "wall", "azim"), P("case", "wall", "azim"), P(), P(), P(), P()),
        out_specs=(P(None, "case", "wall", "azim"), P("case", "azim")),
        check_vma=False,
    )
```

```python
import functools

import jax
import jax.numpy as jnp
from jax import lax
from jax.experimental import pallas as pl
from jax.experimental.pallas import tpu as pltpu
from jax.sharding import PartitionSpec as P

KERNEL_WEIGHTS = (0.55, 0.45)
KERNEL_RATES = (1.15, 3.4)
COUPLING = 0.1
LOG2E = 1.4426950408889634
COMPS = 12
SPECIES = 11
BANDS = 16
EDGE = 6
COURANT = 12
TILES = 13
HEAT_SLOT = 13
OFFSETS = (1, -1, 2, -2, 3, -3)


def lanes(shape):
    return lax.broadcasted_iota(jnp.int32, shape, len(shape) - 1)


def roll(x, shift):
    return pltpu.roll(x, shift % x.shape[-1], x.ndim - 1)


def pack_kernel(state_ref, courant_ref, block_ref, sems):
    copies = [
        pltpu.make_async_copy(state_ref, block_ref.at[pl.ds(0, COMPS)], sems.at[0]),
        pltpu.make_async_copy(courant_ref, block_ref.at[COURANT], sems.at[1]),
    ]
    for copy in copies:
        copy.start()
    for copy in copies:
        copy.wait()


def edge_tiles(block, lane, extra):
    cols = lane.shape[-1]
    last = jnp.zeros(lane.shape, jnp.float32)
    first = jnp.zeros(lane.shape, jnp.float32)
    for k in range(COMPS + 2):
        if k <= COMPS:
            value = block[k]
        elif extra is not None:
            value = extra
        else:
            continue
        here = (lane >= EDGE * k) & (lane < EDGE * (k + 1))
        last = jnp.where(here, roll(value, EDGE * k - (cols - EDGE)), last)
        first = jnp.where(here, roll(value, EDGE * k), first)
    return last, first


def loop(count, body, carry):
    if count <= 4:
        for i in range(count):
            carry = body(i, carry)
        return carry
    return lax.fori_loop(0, count, body, carry)


def absorb(block, base, rows, cross_ref, share_ref, step_ref, emit_ref):
    hot = block[0]
    hot = hot * hot
    hot = hot * hot
    for r in range(rows):
        step = None
        for k in range(SPECIES):
            term = cross_ref[k] * block[1 + k, pl.ds(r, 1), :]
            step = term if step is None else step + term
        step_ref[base + r] = step
        emit_ref[base + r] = share_ref[...] * step * hot[r : r + 1]


def radiate(rows, step_ref, emit_ref, decay_ref, up_ref, down_ref, net_ref, heat_ref):
    count = step_ref.shape[0]
    parts = count // rows
    cols = step_ref.shape[-1]

    def attenuate(part, before):
        for r in range(rows):
            at = part * rows + r
            step = step_ref[at]
            gap = before + step
            for i, rate in enumerate(KERNEL_RATES):
                decay_ref[i, at] = jnp.exp2(gap * (-0.5 * LOG2E * rate))
            before = step
        return before

    zero = jnp.zeros((BANDS, cols), jnp.float32)
    loop(parts, attenuate, zero)

    ratio = KERNEL_WEIGHTS[1] / KERNEL_WEIGHTS[0]

    def halve(x):
        return x[: BANDS // 2] + x[BANDS // 2 :]

    def sweep(part, carry):
        up0, up1, down0, down1 = carry
        for r in range(rows):
            at = part * rows + r
            emitted = emit_ref[at]
            up0 = up0 * decay_ref[0, at] + emitted
            up1 = up1 * decay_ref[1, at] + emitted
            up_ref[at] = halve(up0 + ratio * up1)
            back = count - 1 - at
            emitted = emit_ref[back]
            down0 = down0 + emitted
            down1 = down1 + emitted
            down_ref[back] = halve(down0 + ratio * down1)
            down0 = down0 * decay_ref[0, back]
            down1 = down1 * decay_ref[1, back]
        return up0, up1, down0, down1

    _, _, down0, down1 = loop(parts, sweep, (zero, zero, zero, zero))
    wall = KERNEL_WEIGHTS[0] * jnp.sum(down0 + ratio * down1, axis=0, keepdims=True)

    def combine(part, carry):
        rows_here = pl.ds(part * rows, rows)
        net = jnp.sum(up_ref[rows_here] - down_ref[rows_here], axis=1)
        net_ref[pl.ds(pl.multiple_of(part * rows + rows, rows), rows), :] = net
        return carry

    loop(parts, combine, 0)
    net_ref[rows - 1 : rows, :] = net_ref[rows : rows + 1, :]
    net_ref[rows + count : rows + count + 1, :] = net_ref[rows + count - 1 : rows + count, :]
    scale = KERNEL_WEIGHTS[0] * count / 2.0
    for part in range(parts):
        first = part * rows + rows
        heat_ref[part] = (net_ref[first - 1 : first - 1 + rows, :] - net_ref[first + 1 : first + 1 + rows, :]) * scale
    return wall


def arrive_kernel(slot, block_ref, cross_ref, share_ref, *refs):
    step_ref, emit_ref, outer_ref, inner_ref = refs[-4:]
    rows, cols = block_ref.shape[-2:]
    lane = lanes((rows, cols))
    me = lax.axis_index("wall")
    odd = lax.rem(lax.axis_index("azim"), 2) == 1

    def take(block, slot):
        absorb(block, (me ^ slot) * rows, rows, cross_ref, share_ref, step_ref, emit_ref)
        last, first = edge_tiles(block, lane, None)
        outer_ref[slot] = jnp.where(odd, last, first)
        inner_ref[slot] = jnp.where(odd, first, last)

    if len(block_ref.shape) == 3:
        take(block_ref, slot)
    else:

        def body(i, carry):
            take(block_ref.at[i], i)
            return carry

        loop(block_ref.shape[0], body, 0)


def first_kernel(step_ref, emit_ref, outer_in_ref, inner_in_ref, heating_ref, wall_ref, outer_ref, inner_ref, *scratch):
    heat_ref = scratch[-1]
    parts, rows, cols = heating_ref.shape
    me = lax.axis_index("wall")
    wall_ref[...] = radiate(rows, step_ref, emit_ref, *scratch)
    lane = lanes((rows, cols))
    odd = lax.rem(lax.axis_index("azim"), 2) == 1
    for s in range(parts):
        heating_ref[s] = heat_ref[me ^ s]
        outer_ref[s] = outer_in_ref[s]
        inner_ref[s] = inner_in_ref[s]
    here = (lane >= EDGE * HEAT_SLOT) & (lane < EDGE * (HEAT_SLOT + 1))
    own = heat_ref[me]
    last = roll(own, EDGE * HEAT_SLOT - (cols - EDGE))
    first = roll(own, EDGE * HEAT_SLOT)
    outer_ref[0] = jnp.where(here, jnp.where(odd, last, first), outer_ref[0])
    inner_ref[0] = jnp.where(here, jnp.where(odd, first, last), inner_ref[0])


def coefficients(courant):
    return (0.3 - 0.75 * courant, 0.3 + 0.75 * courant, 0.15 * courant - 0.12, -0.12 - 0.15 * courant, 0.02 - courant / 60.0, 0.02 + courant / 60.0)


def stencil(value, halo, factors, lane, cols):
    total = 0.6 * value
    for offset, factor in zip(OFFSETS, factors):
        if halo is None:
            source = value
        elif offset > 0:
            source = jnp.where(lane < offset, halo, value)
        else:
            source = jnp.where(lane >= cols + offset, halo, value)
        total = total + factor * roll(source, -offset)
    return total


def advance_kernel(ids, *refs):
    slots = refs[: len(ids)]
    heating_ref, outer_ref, inner_ref, middle_ref, edge_ref, halo_ref, near_ref = refs[len(ids) :]
    parts = heating_ref.shape[0]
    own = slots[0] if len(ids) > 1 else slots[0].at[0]
    tile = heating_ref.shape[1:]
    rows, cols = tile
    half = cols // 2
    lane = lanes(tile)
    three = EDGE // 2
    first_half = lax.rem(lane, EDGE) < three
    odd = lax.rem(lax.axis_index("azim"), 2) == 1

    def received(s):
        outer, inner = outer_ref[s], inner_ref[s]
        return jnp.where(odd, inner, outer), jnp.where(odd, outer, inner)

    def place(s, carry):
        left, right = received(s)
        both = jnp.where(first_half, roll(left, -three), roll(right, three))
        for k in range(COMPS):
            halo_ref[s, k] = roll(both, -(EDGE * k + three))
        return carry

    loop(parts, place, 0)

    left, right = received(0)
    for k in range(HEAT_SLOT + 1):
        from_left = roll(left, half - EDGE - EDGE * k)
        from_right = roll(right, -EDGE * k)
        inner = from_left
        if k < COMPS:
            value = own[k]
            inner = jnp.where(lane < half, from_left, jnp.where(lane < half + half // 2, roll(value, half), value))
        near_ref[k] = jnp.where(lane < EDGE, from_right, inner)

    def advance(block, s):
        factors = coefficients(block[COURANT])
        for k in range(COMPS):
            moved = stencil(block[k], halo_ref[s, k], factors, lane, cols)
            if k == 0:
                moved = moved + COUPLING * heating_ref[s]
            middle_ref[s, k] = moved

    if len(ids) > 1:
        for block, slot in zip(slots, ids):
            advance(block, slot)
    else:

        def body(s, carry):
            advance(slots[0].at[s], s)
            return carry

        loop(parts, body, 0)

    factors = coefficients(near_ref[COURANT])
    for k in range(COMPS):
        moved = stencil(near_ref[k], None, factors, lane, cols)
        if k == 0:
            moved = moved + COUPLING * near_ref[HEAT_SLOT]
        halo_ref[0, k] = moved
    for k in range(COMPS):
        moved = halo_ref[0, k]
        edge_ref[k] = jnp.where(lane < half // 2, moved, roll(moved, half))


def last_kernel(block_ref, middle_ref, edge_ref, wall_in_ref, cross_ref, share_ref, out_ref, wall_ref, *scratch):
    heat_ref = scratch[-1]
    own = block_ref if len(block_ref.shape) == 3 else block_ref.at[0]
    rows, cols = out_ref.shape[1:]
    lane = lanes((rows, cols))
    me = lax.axis_index("wall")
    step_ref, emit_ref = scratch[:2]

    def take(slot, carry):
        absorb(middle_ref.at[slot], (me ^ slot) * rows, rows, cross_ref, share_ref, step_ref, emit_ref)
        return carry

    loop(middle_ref.shape[0], take, 0)
    wall = radiate(rows, *scratch)
    wall_ref[...] = 0.5 * (wall_in_ref[...] + wall)
    factors = coefficients(own[COURANT])
    for k in range(COMPS):
        moved = stencil(middle_ref[0, k], edge_ref[k], factors, lane, cols)
        if k == 0:
            moved = moved + COUPLING * heat_ref[me]
        out_ref[k] = 0.5 * (own[k] + moved)


def band_tables(absorb_index, band_index, cross_sections, band_fractions, height, cols):
    entries = cross_sections.shape[0]
    table_slots = lax.broadcasted_iota(jnp.int32, (1, 1, entries), 2)
    area = jnp.sum(jnp.where(absorb_index[:, :, None] == table_slots, cross_sections[None, None, :], 0.0), axis=2)
    share = jnp.sum(jnp.where(band_index[:, None] == table_slots[0], band_fractions[None, :], 0.0), axis=1)
    area = jnp.broadcast_to((area * height)[:, :, None], area.shape + (cols,))
    return area, jnp.broadcast_to(share[:, None], share.shape + (cols,))


def exchange(x, axis, distance):
    return lax.ppermute(x, axis, [(i, i ^ distance) for i in range(lax.axis_size(axis))])


EXCHANGES = (1, 2, 3)


def gather_lines(block):
    count = lax.axis_size("wall")
    if count == 4:
        return [block] + [exchange(block, "wall", s) for s in EXCHANGES], (0,) + EXCHANGES
    stack = block[None]
    for step in range(count.bit_length() - 1):
        stack = jnp.concatenate([stack, exchange(stack, "wall", 1 << step)])
    return [stack], (0,)


VMEM = pl.BlockSpec(memory_space=pltpu.VMEM)


def call(kernel, outs, scratch, *args, aliases=None, limit=32 * 1024 * 1024):
    return pl.pallas_call(
        kernel,
        out_shape=[jax.ShapeDtypeStruct(shape, jnp.float32) for shape in outs],
        in_specs=[VMEM] * len(args),
        out_specs=[VMEM] * len(outs),
        scratch_shapes=[pltpu.VMEM(shape, jnp.float32) for shape in scratch],
        input_output_aliases=aliases or {},
        compiler_params=pltpu.CompilerParams(vmem_limit_bytes=limit),
    )(*args)


def local(state, courant, cross_sections, band_fractions, absorb_index, band_index):
    comps, stations, rows, cols = state.shape
    parts = lax.axis_size("wall")
    count = parts * rows
    ring = lax.axis_size("azim")
    tile = (rows, cols)
    block = jnp.concatenate([state.reshape(comps, rows, cols), courant.reshape((1,) + tile)])
    cross, share = band_tables(absorb_index, band_index, cross_sections, band_fractions, 1.0 / count, cols)
    blocks, ids = gather_lines(block)
    deep = (count, BANDS, cols)
    flat = (count, BANDS // 2, cols)
    whole = (parts,) + tile
    state_of = [deep, deep, whole, whole]
    held = []
    for received, slot in zip(blocks, ids):
        held = call(
            functools.partial(arrive_kernel, slot), state_of, [], received, cross, share, *held,
            aliases={3 + j: j for j in range(len(held))},
        )
    scratch = [(2,) + deep, flat, flat, (count + 2 * rows, cols), whole]
    heating, wall, outer, inner = call(first_kernel, [whole, (1, cols), whole, whole], scratch, *held)
    inner = lax.ppermute(inner, "azim", [(i, i ^ 1) for i in range(ring)])
    outer = lax.ppermute(outer, "azim", [(i, (i + 1) % ring if i % 2 else (i - 1) % ring) for i in range(ring)])
    middle, edge = call(
        functools.partial(advance_kernel, ids),
        [(parts, comps) + tile, (comps,) + tile],
        [(parts, comps) + tile, (HEAT_SLOT + 1,) + tile],
        *blocks, heating, outer, inner,
    )
    new_state, wall = call(
        last_kernel, [(comps,) + tile, (1, cols)], [deep, deep] + scratch,
        blocks[0], middle, edge, wall, cross, share,
    )
    return new_state.reshape(state.shape), wall


def solution(mesh):
    return jax.shard_map(
        local,
        mesh=mesh,
        in_specs=(P(None, "case", "wall", "azim"), P("case", "wall", "azim"), P(), P(), P(), P()),
        out_specs=(P(None, "case", "wall", "azim"), P("case", "azim")),
        check_vma=False,
    )
```

```python
import functools

import jax
import jax.numpy as jnp
from jax import lax
from jax.experimental import pallas as pl
from jax.experimental.pallas import tpu as pltpu
from jax.sharding import PartitionSpec as P

KERNEL_WEIGHTS = (0.55, 0.45)
KERNEL_RATES = (1.15, 3.4)
COUPLING = 0.1
LOG2E = 1.4426950408889634
COMPS = 12
SPECIES = 11
BANDS = 16
EDGE = 6
COURANT = 12
TILES = 13
PACKED = EDGE * COMPS
HEAT_AT = 96
OFFSETS = (1, -1, 2, -2, 3, -3)


def lanes(shape):
    return lax.broadcasted_iota(jnp.int32, shape, len(shape) - 1)


def roll(x, shift):
    return pltpu.roll(x, shift % x.shape[-1], x.ndim - 1)


def pack_kernel(state_ref, courant_ref, block_ref, sems):
    copies = [
        pltpu.make_async_copy(state_ref, block_ref.at[pl.ds(0, COMPS)], sems.at[0]),
        pltpu.make_async_copy(courant_ref, block_ref.at[COURANT], sems.at[1]),
    ]
    for copy in copies:
        copy.start()
    for copy in copies:
        copy.wait()


def edge_tiles(block, lane):
    cols = lane.shape[-1]
    last = jnp.zeros(lane.shape, jnp.float32)
    first = jnp.zeros(lane.shape, jnp.float32)
    for k in range(COMPS):
        here = (lane >= EDGE * k) & (lane < EDGE * (k + 1))
        last = jnp.where(here, roll(block[k], EDGE * k - (cols - EDGE)), last)
        first = jnp.where(here, roll(block[k], EDGE * k), first)
    return last, first


def spread(value, lane):
    group = jnp.where(lane < EDGE, roll(value, EDGE // 2), 0.0)
    for width in (1, 2, 4, 8):
        group = group + roll(group, EDGE * width)
    return group


def loop(count, body, carry):
    if count <= 4:
        for i in range(count):
            carry = body(i, carry)
        return carry
    return lax.fori_loop(0, count, body, carry)


def absorb(block, base, rows, cross_ref, share_ref, step_ref, emit_ref):
    hot = block[0]
    hot = hot * hot
    hot = hot * hot
    for r in range(rows):
        step = None
        for k in range(SPECIES):
            term = cross_ref[k] * block[1 + k, pl.ds(r, 1), :]
            step = term if step is None else step + term
        step_ref[base + r] = step
        emit_ref[base + r] = share_ref[...] * step * hot[r : r + 1]


def radiate(rows, step_ref, emit_ref, decay_ref, up_ref, down_ref, net_ref, heat_ref):
    count = step_ref.shape[0]
    parts = count // rows
    cols = step_ref.shape[-1]

    def attenuate(part, before):
        for r in range(rows):
            at = part * rows + r
            step = step_ref[at]
            gap = before + step
            for i, rate in enumerate(KERNEL_RATES):
                decay_ref[i, at] = jnp.exp2(gap * (-0.5 * LOG2E * rate))
            before = step
        return before

    zero = jnp.zeros((BANDS, cols), jnp.float32)
    loop(parts, attenuate, zero)

    ratio = KERNEL_WEIGHTS[1] / KERNEL_WEIGHTS[0]

    def halve(x):
        return x[: BANDS // 2] + x[BANDS // 2 :]

    def sweep(part, carry):
        up0, up1, down0, down1 = carry
        for r in range(rows):
            at = part * rows + r
            emitted = emit_ref[at]
            up0 = up0 * decay_ref[0, at] + emitted
            up1 = up1 * decay_ref[1, at] + emitted
            up_ref[at] = halve(up0 + ratio * up1)
            back = count - 1 - at
            emitted = emit_ref[back]
            down0 = down0 + emitted
            down1 = down1 + emitted
            down_ref[back] = halve(down0 + ratio * down1)
            down0 = down0 * decay_ref[0, back]
            down1 = down1 * decay_ref[1, back]
        return up0, up1, down0, down1

    _, _, down0, down1 = loop(parts, sweep, (zero, zero, zero, zero))
    wall = KERNEL_WEIGHTS[0] * jnp.sum(down0 + ratio * down1, axis=0, keepdims=True)

    def combine(part, carry):
        rows_here = pl.ds(part * rows, rows)
        net = jnp.sum(up_ref[rows_here] - down_ref[rows_here], axis=1)
        net_ref[pl.ds(pl.multiple_of(part * rows + rows, rows), rows), :] = net
        return carry

    loop(parts, combine, 0)
    net_ref[rows - 1 : rows, :] = net_ref[rows : rows + 1, :]
    net_ref[rows + count : rows + count + 1, :] = net_ref[rows + count - 1 : rows + count, :]
    scale = KERNEL_WEIGHTS[0] * count / 2.0
    for part in range(parts):
        first = part * rows + rows
        heat_ref[part] = (net_ref[first - 1 : first - 1 + rows, :] - net_ref[first + 1 : first + 1 + rows, :]) * scale
    return wall


def arrive_kernel(slots, block_ref, cross_ref, share_ref, *refs):
    step_ref, emit_ref, outer_ref, inner_ref = refs[-4:]
    rows, cols = block_ref.shape[-2:]
    lane = lanes((rows, cols))
    me = lax.axis_index("wall")
    odd = lax.rem(lax.axis_index("azim"), 2) == 1

    def take(block, slot):
        absorb(block, (me ^ slot) * rows, rows, cross_ref, share_ref, step_ref, emit_ref)
        last, first = edge_tiles(block, lane)
        outer_ref[slot] = jnp.where(odd, last, first)
        inner_ref[slot] = jnp.where(odd, first, last)

    if len(block_ref.shape) == 3:
        take(block_ref, slot_here(slots))
    else:

        def body(i, carry):
            take(block_ref.at[i], i)
            return carry

        loop(block_ref.shape[0], body, 0)
    if slots[0] == 0:
        own = block_ref if len(block_ref.shape) == 3 else block_ref.at[0]
        edges = spread(own[COURANT], lane)
        outer_ref[outer_ref.shape[0] - 1] = edges
        inner_ref[outer_ref.shape[0] - 1] = edges


def first_kernel(step_ref, emit_ref, outer_in_ref, inner_in_ref, heating_ref, wall_ref, outer_ref, inner_ref, *scratch):
    heat_ref = scratch[-1]
    parts, rows, cols = heating_ref.shape
    me = lax.axis_index("wall")
    wall_ref[...] = radiate(rows, step_ref, emit_ref, *scratch)
    lane = lanes((rows, cols))
    for s in range(parts):
        heating_ref[s] = heat_ref[me ^ s]
        outer_ref[s] = outer_in_ref[s]
        inner_ref[s] = inner_in_ref[s]
    here = (lane >= HEAT_AT) & (lane < HEAT_AT + EDGE)
    edges = jnp.where(here, roll(heat_ref[me], EDGE // 2 + HEAT_AT), outer_in_ref[parts])
    outer_ref[parts] = edges
    inner_ref[parts] = edges


def coefficients(courant):
    return (0.3 - 0.75 * courant, 0.3 + 0.75 * courant, 0.15 * courant - 0.12, -0.12 - 0.15 * courant, 0.02 - courant / 60.0, 0.02 + courant / 60.0)


def stencil(value, halo, factors, lane, cols):
    total = 0.6 * value
    for offset, factor in zip(OFFSETS, factors):
        if halo is None:
            source = value
        elif offset > 0:
            source = jnp.where(lane < offset, halo, value)
        else:
            source = jnp.where(lane >= cols + offset, halo, value)
        total = total + factor * roll(source, -offset)
    return total


def center_kernel(ids, *refs):
    blocks = refs[: len(ids)]
    heating_ref, middle_ref, packed_ref = refs[len(ids) :]
    rows, cols = heating_ref.shape[1:]
    lane = lanes((rows, cols))

    def advance(block, s):
        factors = coefficients(block[COURANT])
        packed_ref[s] = spread(block[COURANT], lane)
        for k in range(COMPS):
            moved = stencil(block[k], None, factors, lane, cols)
            if k == 0:
                moved = moved + COUPLING * heating_ref[s]
            middle_ref[s, k] = moved

    if len(ids) > 1:
        for block, slot in zip(blocks, ids):
            advance(block, slot_here(slot))
    else:

        def body(s, carry):
            advance(blocks[0].at[s], s)
            return carry

        loop(heating_ref.shape[0], body, 0)


def border_kernel(middle_in_ref, packed_ref, my_outer_ref, my_inner_ref, outer_ref, inner_ref, middle_ref, edge_ref, change_ref):
    parts, comps, rows, cols = middle_ref.shape
    lane = lanes((rows, cols))
    at = lax.rem(lane, EDGE)
    three = EDGE // 2
    odd = lax.rem(lax.axis_index("azim"), 2) == 1

    def sides(s):
        outer, inner = outer_ref[s], inner_ref[s]
        my_outer, my_inner = my_outer_ref[s], my_inner_ref[s]
        return (
            jnp.where(odd, inner, outer), jnp.where(odd, outer, inner),
            jnp.where(odd, my_outer, my_inner), jnp.where(odd, my_inner, my_outer),
        )

    def differ(s, carry):
        left, right, last, first = sides(s)
        left, right = left - last, right - first
        factors = coefficients(packed_ref[s])
        change = jnp.zeros((rows, cols), jnp.float32)
        for reach in range(1, three + 1):
            ahead = factors[2 * reach - 2] * roll(right, three - reach)
            behind = factors[2 * reach - 1] * roll(left, reach - three)
            ahead = jnp.where((at >= three - reach) & (at < three), ahead, 0.0)
            change = change + jnp.where((at >= three) & (at < three + reach), behind, ahead)
        change_ref[s] = change
        return carry

    loop(parts, differ, 0)

    left, right, last, first = sides(0)
    outside = jnp.where(at < three, jnp.where(odd, inner_ref[parts], outer_ref[parts]), jnp.where(odd, outer_ref[parts], inner_ref[parts]))
    factors = dict(zip(OFFSETS, coefficients(outside)))
    factors[0] = 0.6
    edge = jnp.where(lane < EDGE, COUPLING * roll(outside, -HEAT_AT), 0.0)
    for offset in range(-three, three + 1):
        behind = roll(jnp.where(at <= EDGE - 1 + offset, left, last), -(three + offset))
        ahead = roll(jnp.where(at < offset, first, right), three - offset)
        edge = edge + factors[offset] * jnp.where(at <= three - 1 - offset, behind, ahead)
    change_ref[parts] = edge

    border = (lane < three) | (lane >= cols - three)

    def mend(s, carry):
        change = change_ref[s]
        for k in range(COMPS):
            middle_ref[s, k] = middle_in_ref[s, k] + jnp.where(border, roll(change, -(EDGE * k + three)), 0.0)
        return carry

    loop(parts, mend, 0)
    edge = change_ref[parts]
    for k in range(COMPS):
        edge_ref[k] = roll(edge, -(EDGE * k + three))


def last_kernel(block_ref, middle_ref, edge_ref, wall_in_ref, cross_ref, share_ref, out_ref, wall_ref, *scratch):
    heat_ref = scratch[-1]
    own = block_ref if len(block_ref.shape) == 3 else block_ref.at[0]
    rows, cols = out_ref.shape[1:]
    lane = lanes((rows, cols))
    me = lax.axis_index("wall")
    step_ref, emit_ref = scratch[:2]

    def take(slot, carry):
        absorb(middle_ref.at[slot], (me ^ slot) * rows, rows, cross_ref, share_ref, step_ref, emit_ref)
        return carry

    loop(middle_ref.shape[0], take, 0)
    wall = radiate(rows, *scratch)
    wall_ref[...] = 0.5 * (wall_in_ref[...] + wall)
    factors = coefficients(own[COURANT])
    for k in range(COMPS):
        moved = stencil(middle_ref[0, k], edge_ref[k], factors, lane, cols)
        if k == 0:
            moved = moved + COUPLING * heat_ref[me]
        out_ref[k] = 0.5 * (own[k] + moved)


def band_tables(absorb_index, band_index, cross_sections, band_fractions, height, cols):
    entries = cross_sections.shape[0]
    table_slots = lax.broadcasted_iota(jnp.int32, (1, 1, entries), 2)
    area = jnp.sum(jnp.where(absorb_index[:, :, None] == table_slots, cross_sections[None, None, :], 0.0), axis=2)
    share = jnp.sum(jnp.where(band_index[:, None] == table_slots[0], band_fractions[None, :], 0.0), axis=1)
    area = jnp.broadcast_to((area * height)[:, :, None], area.shape + (cols,))
    return area, jnp.broadcast_to(share[:, None], share.shape + (cols,))


def exchange(x, axis, distance):
    return lax.ppermute(x, axis, [(i, i ^ distance) for i in range(lax.axis_size(axis))])


EXCHANGES = ((1, 0, 3, 2), (3, 2, 0, 1), (2, 3, 1, 0))


def gather_lines(block):
    count = lax.axis_size("wall")
    if count == 4:
        blocks, slots = [block], [(0,) * count]
        for targets in EXCHANGES:
            blocks.append(lax.ppermute(block, "wall", list(enumerate(targets))))
            slots.append(tuple(w ^ targets.index(w) for w in range(count)))
        return blocks, tuple(slots)
    stack = block[None]
    for step in range(count.bit_length() - 1):
        stack = jnp.concatenate([stack, exchange(stack, "wall", 1 << step)])
    return [stack], ((0,) * count,)


def slot_here(slots):
    me = lax.axis_index("wall")
    if len(set(slots)) == 1:
        return slots[0]
    return sum(jnp.where(me == w, slot, 0) for w, slot in enumerate(slots))


VMEM = pl.BlockSpec(memory_space=pltpu.VMEM)


def call(kernel, outs, scratch, *args, aliases=None, limit=32 * 1024 * 1024):
    return pl.pallas_call(
        kernel,
        out_shape=[jax.ShapeDtypeStruct(shape, jnp.float32) for shape in outs],
        in_specs=[VMEM] * len(args),
        out_specs=[VMEM] * len(outs),
        scratch_shapes=[pltpu.VMEM(shape, jnp.float32) for shape in scratch],
        input_output_aliases=aliases or {},
        compiler_params=pltpu.CompilerParams(vmem_limit_bytes=limit),
    )(*args)


def local(state, courant, cross_sections, band_fractions, absorb_index, band_index):
    comps, stations, rows, cols = state.shape
    parts = lax.axis_size("wall")
    count = parts * rows
    ring = lax.axis_size("azim")
    tile = (rows, cols)
    block = jnp.concatenate([state.reshape(comps, rows, cols), courant.reshape((1,) + tile)])
    cross, share = band_tables(absorb_index, band_index, cross_sections, band_fractions, 1.0 / count, cols)
    blocks, ids = gather_lines(block)
    deep = (count, BANDS, cols)
    flat = (count, BANDS // 2, cols)
    whole = (parts,) + tile
    message = (parts + 1,) + tile
    state_of = [deep, deep, message, message]
    held = []
    for received, slot in zip(blocks, ids):
        held = call(
            functools.partial(arrive_kernel, slot), state_of, [], received, cross, share, *held,
            aliases={3 + j: j for j in range(len(held))},
        )
    scratch = [(2,) + deep, flat, flat, (count + 2 * rows, cols), whole]
    heating, wall, my_outer, my_inner = call(first_kernel, [whole, (1, cols), message, message], scratch, *held)
    inner = lax.ppermute(my_inner, "azim", [(i, i ^ 1) for i in range(ring)])
    outer = lax.ppermute(my_outer, "azim", [(i, (i + 1) % ring if i % 2 else (i - 1) % ring) for i in range(ring)])
    middle, packed = call(
        functools.partial(center_kernel, ids), [(parts, comps) + tile, whole], [], *blocks, heating,
    )
    middle, edge = call(
        border_kernel, [(parts, comps) + tile, (comps,) + tile], [message],
        middle, packed, my_outer, my_inner, outer, inner, aliases={0: 0},
    )
    new_state, wall = call(
        last_kernel, [(comps,) + tile, (1, cols)], [deep, deep] + scratch,
        blocks[0], middle, edge, wall, cross, share,
    )
    return new_state.reshape(state.shape), wall


def solution(mesh):
    return jax.shard_map(
        local,
        mesh=mesh,
        in_specs=(P(None, "case", "wall", "azim"), P("case", "wall", "azim"), P(), P(), P(), P()),
        out_specs=(P(None, "case", "wall", "azim"), P("case", "azim")),
        check_vma=False,
    )
```

```python
import functools

import jax
import jax.numpy as jnp
from jax import lax
from jax.experimental import pallas as pl
from jax.experimental.pallas import tpu as pltpu
from jax.sharding import PartitionSpec as P

KERNEL_WEIGHTS = (0.55, 0.45)
KERNEL_RATES = (1.15, 3.4)
COUPLING = 0.1
LOG2E = 1.4426950408889634
COMPS = 12
SPECIES = 11
BANDS = 16
EDGE = 6
COURANT = 12
TILES = 13
PACKED = EDGE * COMPS
HEAT_AT = 96
OFFSETS = (1, -1, 2, -2, 3, -3)


def lanes(shape):
    return lax.broadcasted_iota(jnp.int32, shape, len(shape) - 1)


def roll(x, shift):
    return pltpu.roll(x, shift % x.shape[-1], x.ndim - 1)


def pack_kernel(state_ref, courant_ref, block_ref, sems):
    copies = [
        pltpu.make_async_copy(state_ref, block_ref.at[pl.ds(0, COMPS)], sems.at[0]),
        pltpu.make_async_copy(courant_ref, block_ref.at[COURANT], sems.at[1]),
    ]
    for copy in copies:
        copy.start()
    for copy in copies:
        copy.wait()


def edge_tiles(block, lane):
    cols = lane.shape[-1]
    last = jnp.zeros(lane.shape, jnp.float32)
    first = jnp.zeros(lane.shape, jnp.float32)
    for k in range(COMPS):
        here = (lane >= EDGE * k) & (lane < EDGE * (k + 1))
        last = jnp.where(here, roll(block[k], EDGE * k - (cols - EDGE)), last)
        first = jnp.where(here, roll(block[k], EDGE * k), first)
    return last, first


def spread(value, lane):
    group = jnp.where(lane < EDGE, roll(value, EDGE // 2), 0.0)
    for width in (1, 2, 4, 8):
        group = group + roll(group, EDGE * width)
    return group


def loop(count, body, carry):
    if count <= 4:
        for i in range(count):
            carry = body(i, carry)
        return carry
    return lax.fori_loop(0, count, body, carry)


def absorb(block, base, rows, cross_ref, share_ref, step_ref, emit_ref):
    hot = block[0]
    hot = hot * hot
    hot = hot * hot
    for r in range(rows):
        step = None
        for k in range(SPECIES):
            term = cross_ref[k] * block[1 + k, pl.ds(r, 1), :]
            step = term if step is None else step + term
        step_ref[base + r] = step
        emit_ref[base + r] = share_ref[...] * step * hot[r : r + 1]


def radiate(rows, step_ref, emit_ref, decay_ref, up_ref, down_ref, net_ref, heat_ref):
    count = step_ref.shape[0]
    parts = count // rows
    cols = step_ref.shape[-1]

    def attenuate(part, before):
        for r in range(rows):
            at = part * rows + r
            step = step_ref[at]
            gap = before + step
            for i, rate in enumerate(KERNEL_RATES):
                decay_ref[i, at] = jnp.exp2(gap * (-0.5 * LOG2E * rate))
            before = step
        return before

    zero = jnp.zeros((BANDS, cols), jnp.float32)
    loop(parts, attenuate, zero)

    ratio = KERNEL_WEIGHTS[1] / KERNEL_WEIGHTS[0]

    def halve(x):
        return x[: BANDS // 2] + x[BANDS // 2 :]

    def sweep(part, carry):
        up0, up1, down0, down1 = carry
        for r in range(rows):
            at = part * rows + r
            emitted = emit_ref[at]
            up0 = up0 * decay_ref[0, at] + emitted
            up1 = up1 * decay_ref[1, at] + emitted
            up_ref[at] = halve(up0 + ratio * up1)
            back = count - 1 - at
            emitted = emit_ref[back]
            down0 = down0 + emitted
            down1 = down1 + emitted
            down_ref[back] = halve(down0 + ratio * down1)
            down0 = down0 * decay_ref[0, back]
            down1 = down1 * decay_ref[1, back]
        return up0, up1, down0, down1

    _, _, down0, down1 = loop(parts, sweep, (zero, zero, zero, zero))
    wall = KERNEL_WEIGHTS[0] * jnp.sum(down0 + ratio * down1, axis=0, keepdims=True)

    def combine(part, carry):
        rows_here = pl.ds(part * rows, rows)
        net = jnp.sum(up_ref[rows_here] - down_ref[rows_here], axis=1)
        net_ref[pl.ds(pl.multiple_of(part * rows + rows, rows), rows), :] = net
        return carry

    loop(parts, combine, 0)
    net_ref[rows - 1 : rows, :] = net_ref[rows : rows + 1, :]
    net_ref[rows + count : rows + count + 1, :] = net_ref[rows + count - 1 : rows + count, :]
    scale = KERNEL_WEIGHTS[0] * count / 2.0
    for part in range(parts):
        first = part * rows + rows
        heat_ref[part] = (net_ref[first - 1 : first - 1 + rows, :] - net_ref[first + 1 : first + 1 + rows, :]) * scale
    return wall


def arrive_kernel(slots, block_ref, cross_ref, share_ref, *refs):
    step_ref, emit_ref, outer_ref, inner_ref = refs[-4:]
    rows, cols = block_ref.shape[-2:]
    lane = lanes((rows, cols))
    me = lax.axis_index("wall")
    odd = lax.rem(lax.axis_index("azim"), 2) == 1

    def take(block, slot):
        absorb(block, (me ^ slot) * rows, rows, cross_ref, share_ref, step_ref, emit_ref)
        last, first = edge_tiles(block, lane)
        outer_ref[slot] = jnp.where(odd, last, first)
        inner_ref[slot] = jnp.where(odd, first, last)

    if len(block_ref.shape) == 3:
        take(block_ref, slot_here(slots))
    else:

        def body(i, carry):
            take(block_ref.at[i], i)
            return carry

        loop(block_ref.shape[0], body, 0)
    if slots[0] == 0:
        own = block_ref if len(block_ref.shape) == 3 else block_ref.at[0]
        edges = spread(own[COURANT], lane)
        outer_ref[outer_ref.shape[0] - 1] = edges
        inner_ref[outer_ref.shape[0] - 1] = edges


def first_kernel(step_ref, emit_ref, outer_in_ref, inner_in_ref, heating_ref, wall_ref, outer_ref, inner_ref, *scratch):
    heat_ref = scratch[-1]
    parts, rows, cols = heating_ref.shape
    me = lax.axis_index("wall")
    wall_ref[...] = radiate(rows, step_ref, emit_ref, *scratch)
    lane = lanes((rows, cols))
    for s in range(parts):
        heating_ref[s] = heat_ref[me ^ s]
        outer_ref[s] = outer_in_ref[s]
        inner_ref[s] = inner_in_ref[s]
    here = (lane >= HEAT_AT) & (lane < HEAT_AT + EDGE)
    edges = jnp.where(here, roll(heat_ref[me], EDGE // 2 + HEAT_AT), outer_in_ref[parts])
    outer_ref[parts] = edges
    inner_ref[parts] = edges


def coefficients(courant):
    return (0.3 - 0.75 * courant, 0.3 + 0.75 * courant, 0.15 * courant - 0.12, -0.12 - 0.15 * courant, 0.02 - courant / 60.0, 0.02 + courant / 60.0)


def stencil(value, halo, factors, lane, cols):
    total = 0.6 * value
    for offset, factor in zip(OFFSETS, factors):
        if halo is None:
            source = value
        elif offset > 0:
            source = jnp.where(lane < offset, halo, value)
        else:
            source = jnp.where(lane >= cols + offset, halo, value)
        total = total + factor * roll(source, -offset)
    return total


def center_kernel(ids, *refs):
    blocks = refs[: len(ids)]
    heating_ref, middle_ref, packed_ref = refs[len(ids) :]
    rows, cols = heating_ref.shape[1:]
    lane = lanes((rows, cols))

    def advance(block, s):
        factors = coefficients(block[COURANT])
        packed_ref[s] = spread(block[COURANT], lane)
        for k in range(COMPS):
            moved = stencil(block[k], None, factors, lane, cols)
            if k == 0:
                moved = moved + COUPLING * heating_ref[s]
            middle_ref[s, k] = moved

    if len(ids) > 1:
        for block, slot in zip(blocks, ids):
            advance(block, slot_here(slot))
    else:

        def body(s, carry):
            advance(blocks[0].at[s], s)
            return carry

        loop(heating_ref.shape[0], body, 0)


def border_kernel(middle_in_ref, packed_ref, my_outer_ref, my_inner_ref, outer_ref, inner_ref, middle_ref, edge_ref, change_ref):
    parts, comps, rows, cols = middle_ref.shape
    lane = lanes((rows, cols))
    at = lax.rem(lane, EDGE)
    three = EDGE // 2
    odd = lax.rem(lax.axis_index("azim"), 2) == 1

    def sides(s):
        outer, inner = outer_ref[s], inner_ref[s]
        my_outer, my_inner = my_outer_ref[s], my_inner_ref[s]
        return (
            jnp.where(odd, inner, outer), jnp.where(odd, outer, inner),
            jnp.where(odd, my_outer, my_inner), jnp.where(odd, my_inner, my_outer),
        )

    def differ(s, carry):
        left, right, last, first = sides(s)
        left, right = left - last, right - first
        factors = coefficients(packed_ref[s])
        change = jnp.zeros((rows, cols), jnp.float32)
        for reach in range(1, three + 1):
            ahead = factors[2 * reach - 2] * roll(right, three - reach)
            behind = factors[2 * reach - 1] * roll(left, reach - three)
            ahead = jnp.where((at >= three - reach) & (at < three), ahead, 0.0)
            change = change + jnp.where((at >= three) & (at < three + reach), behind, ahead)
        change_ref[s] = change
        return carry

    loop(parts, differ, 0)

    left, right, last, first = sides(0)
    outside = jnp.where(at < three, jnp.where(odd, inner_ref[parts], outer_ref[parts]), jnp.where(odd, outer_ref[parts], inner_ref[parts]))
    factors = dict(zip(OFFSETS, coefficients(outside)))
    factors[0] = 0.6
    edge = jnp.where(lane < EDGE, COUPLING * roll(outside, -HEAT_AT), 0.0)
    for offset in range(-three, three + 1):
        behind = roll(jnp.where(at <= EDGE - 1 + offset, left, last), -(three + offset))
        ahead = roll(jnp.where(at < offset, first, right), three - offset)
        edge = edge + factors[offset] * jnp.where(at <= three - 1 - offset, behind, ahead)
    change_ref[parts] = edge

    border = (lane < three) | (lane >= cols - three)

    def mend(s, carry):
        change = change_ref[s]
        for k in range(COMPS):
            middle_ref[s, k] = middle_in_ref[s, k] + jnp.where(border, roll(change, -(EDGE * k + three)), 0.0)
        return carry

    loop(parts, mend, 0)
    edge = change_ref[parts]
    for k in range(COMPS):
        edge_ref[k] = roll(edge, -(EDGE * k + three))


def last_kernel(block_ref, middle_ref, edge_ref, wall_in_ref, cross_ref, share_ref, out_ref, wall_ref, *scratch):
    heat_ref = scratch[-1]
    own = block_ref if len(block_ref.shape) == 3 else block_ref.at[0]
    rows, cols = out_ref.shape[1:]
    lane = lanes((rows, cols))
    me = lax.axis_index("wall")
    step_ref, emit_ref = scratch[:2]

    def take(slot, carry):
        absorb(middle_ref.at[slot], (me ^ slot) * rows, rows, cross_ref, share_ref, step_ref, emit_ref)
        return carry

    loop(middle_ref.shape[0], take, 0)
    wall = radiate(rows, *scratch)
    wall_ref[...] = 0.5 * (wall_in_ref[...] + wall)
    factors = coefficients(own[COURANT])
    for k in range(COMPS):
        moved = stencil(middle_ref[0, k], edge_ref[k], factors, lane, cols)
        if k == 0:
            moved = moved + COUPLING * heat_ref[me]
        out_ref[k] = 0.5 * (own[k] + moved)


def band_tables(absorb_index, band_index, cross_sections, band_fractions, height, cols):
    entries = cross_sections.shape[0]
    table_slots = lax.broadcasted_iota(jnp.int32, (1, 1, entries), 2)
    area = jnp.sum(jnp.where(absorb_index[:, :, None] == table_slots, cross_sections[None, None, :], 0.0), axis=2)
    share = jnp.sum(jnp.where(band_index[:, None] == table_slots[0], band_fractions[None, :], 0.0), axis=1)
    area = jnp.broadcast_to((area * height)[:, :, None], area.shape + (cols,))
    return area, jnp.broadcast_to(share[:, None], share.shape + (cols,))


def exchange(x, axis, distance):
    return lax.ppermute(x, axis, [(i, i ^ distance) for i in range(lax.axis_size(axis))])


EXCHANGES = ((1, 2, 3, 0), (2, 3, 0, 1), (3, 0, 1, 2))


def copy_kernel(source_ref, *refs):
    for ref in refs:
        ref[...] = source_ref[...]


def gather_lines(block):
    count = lax.axis_size("wall")
    if count == 4:
        blocks, slots = [block], [(0,) * count]
        copies = list(call(copy_kernel, [block.shape] * 2, [], block))
        for targets in EXCHANGES:
            sent = copies.pop() if copies and targets != EXCHANGES[0] else block
            blocks.append(lax.ppermute(sent, "wall", list(enumerate(targets))))
            slots.append(tuple(w ^ targets.index(w) for w in range(count)))
        return blocks, tuple(slots)
    stack = block[None]
    for step in range(count.bit_length() - 1):
        stack = jnp.concatenate([stack, exchange(stack, "wall", 1 << step)])
    return [stack], ((0,) * count,)


def slot_here(slots):
    me = lax.axis_index("wall")
    if len(set(slots)) == 1:
        return slots[0]
    return sum(jnp.where(me == w, slot, 0) for w, slot in enumerate(slots))


VMEM = pl.BlockSpec(memory_space=pltpu.VMEM)


def call(kernel, outs, scratch, *args, aliases=None, limit=32 * 1024 * 1024):
    return pl.pallas_call(
        kernel,
        out_shape=[jax.ShapeDtypeStruct(shape, jnp.float32) for shape in outs],
        in_specs=[VMEM] * len(args),
        out_specs=[VMEM] * len(outs),
        scratch_shapes=[pltpu.VMEM(shape, jnp.float32) for shape in scratch],
        input_output_aliases=aliases or {},
        compiler_params=pltpu.CompilerParams(vmem_limit_bytes=limit),
    )(*args)


def local(state, courant, cross_sections, band_fractions, absorb_index, band_index):
    comps, stations, rows, cols = state.shape
    parts = lax.axis_size("wall")
    count = parts * rows
    ring = lax.axis_size("azim")
    tile = (rows, cols)
    block = jnp.concatenate([state.reshape(comps, rows, cols), courant.reshape((1,) + tile)])
    cross, share = band_tables(absorb_index, band_index, cross_sections, band_fractions, 1.0 / count, cols)
    blocks, ids = gather_lines(block)
    deep = (count, BANDS, cols)
    flat = (count, BANDS // 2, cols)
    whole = (parts,) + tile
    message = (parts + 1,) + tile
    state_of = [deep, deep, message, message]
    held = []
    for received, slot in zip(blocks, ids):
        held = call(
            functools.partial(arrive_kernel, slot), state_of, [], received, cross, share, *held,
            aliases={3 + j: j for j in range(len(held))},
        )
    scratch = [(2,) + deep, flat, flat, (count + 2 * rows, cols), whole]
    heating, wall, my_outer, my_inner = call(first_kernel, [whole, (1, cols), message, message], scratch, *held)
    inner = lax.ppermute(my_inner, "azim", [(i, i ^ 1) for i in range(ring)])
    outer = lax.ppermute(my_outer, "azim", [(i, (i + 1) % ring if i % 2 else (i - 1) % ring) for i in range(ring)])
    middle, packed = call(
        functools.partial(center_kernel, ids), [(parts, comps) + tile, whole], [], *blocks, heating,
    )
    middle, edge = call(
        border_kernel, [(parts, comps) + tile, (comps,) + tile], [message],
        middle, packed, my_outer, my_inner, outer, inner, aliases={0: 0},
    )
    new_state, wall = call(
        last_kernel, [(comps,) + tile, (1, cols)], [deep, deep] + scratch,
        blocks[0], middle, edge, wall, cross, share,
    )
    return new_state.reshape(state.shape), wall


def solution(mesh):
    return jax.shard_map(
        local,
        mesh=mesh,
        in_specs=(P(None, "case", "wall", "azim"), P("case", "wall", "azim"), P(), P(), P(), P()),
        out_specs=(P(None, "case", "wall", "azim"), P("case", "azim")),
        check_vma=False,
    )
```

```python
import functools

import jax
import jax.numpy as jnp
from jax import lax
from jax.experimental import pallas as pl
from jax.experimental.pallas import tpu as pltpu
from jax.sharding import PartitionSpec as P

KERNEL_WEIGHTS = (0.55, 0.45)
KERNEL_RATES = (1.15, 3.4)
COUPLING = 0.1
LOG2E = 1.4426950408889634
COMPS = 12
SPECIES = 11
BANDS = 16
EDGE = 6
COURANT = 12
PIECES = 3
TILES = 13
PACKED = EDGE * COMPS
HEAT_AT = PACKED + 8 * EDGE
OFFSETS = (1, -1, 2, -2, 3, -3)


def lanes(shape):
    return lax.broadcasted_iota(jnp.int32, shape, len(shape) - 1)


def roll(x, shift):
    return pltpu.roll(x, shift % x.shape[-1], x.ndim - 1)


def pack_kernel(state_ref, courant_ref, block_ref, sems):
    copies = [pltpu.make_async_copy(courant_ref, block_ref.at[COURANT], sems.at[PIECES])]
    for i in range(PIECES):
        piece = pl.ds(i * (COMPS // PIECES), COMPS // PIECES)
        copies.append(pltpu.make_async_copy(state_ref.at[piece], block_ref.at[piece], sems.at[i]))
    for copy in copies:
        copy.start()
    for copy in copies:
        copy.wait()


def edge_tiles(block, lane):
    cols = lane.shape[-1]
    last = jnp.zeros(lane.shape, jnp.float32)
    first = jnp.zeros(lane.shape, jnp.float32)
    for k in range(COMPS):
        here = (lane >= EDGE * k) & (lane < EDGE * (k + 1))
        last = jnp.where(here, roll(block[k], EDGE * k - (cols - EDGE)), last)
        first = jnp.where(here, roll(block[k], EDGE * k), first)
    return last, first


def spread(value, lane, start, widths):
    group = jnp.where((lane >= start) & (lane < start + EDGE), roll(value, EDGE // 2 + start), 0.0)
    for width in widths:
        group = group + roll(group, EDGE * width)
    return group


def loop(count, body, carry):
    if count <= 4:
        for i in range(count):
            carry = body(i, carry)
        return carry
    return lax.fori_loop(0, count, body, carry)


def decay(gap, decay_ref, at):
    for i, rate in enumerate(KERNEL_RATES):
        decay_ref[i, at] = jnp.exp2(gap * (-0.5 * LOG2E * rate))


def absorb(block, base, rows, cross_ref, share_ref, step_ref, emit_ref, decay_ref):
    hot = block[0]
    hot = hot * hot
    hot = hot * hot
    before = None
    for r in range(rows):
        step = None
        for k in range(SPECIES):
            term = cross_ref[k] * block[1 + k, pl.ds(r, 1), :]
            step = term if step is None else step + term
        if r in (0, rows - 1):
            step_ref[base // rows, min(r, 1)] = step
        emit_ref[base + r] = share_ref[...] * step * hot[r : r + 1]
        if r:
            decay(before + step, decay_ref, base + r)
        before = step


def radiate(rows, step_ref, emit_ref, decay_ref, up_ref, down_ref, net_ref, heat_ref):
    count = emit_ref.shape[0]
    parts = count // rows
    cols = emit_ref.shape[-1]

    zero = jnp.zeros((BANDS, cols), jnp.float32)

    def attenuate(part, before):
        decay(before + step_ref[part, 0], decay_ref, part * rows)
        return step_ref[part, 1]

    loop(parts, attenuate, zero)

    ratio = KERNEL_WEIGHTS[1] / KERNEL_WEIGHTS[0]

    def halve(x):
        return x[: BANDS // 2] + x[BANDS // 2 :]

    def sweep(part, carry):
        up0, up1, down0, down1 = carry
        for r in range(rows):
            at = part * rows + r
            emitted = emit_ref[at]
            up0 = up0 * decay_ref[0, at] + emitted
            up1 = up1 * decay_ref[1, at] + emitted
            up_ref[at] = halve(up0 + ratio * up1)
            back = count - 1 - at
            emitted = emit_ref[back]
            down0 = down0 + emitted
            down1 = down1 + emitted
            down_ref[back] = halve(down0 + ratio * down1)
            down0 = down0 * decay_ref[0, back]
            down1 = down1 * decay_ref[1, back]
        return up0, up1, down0, down1

    _, _, down0, down1 = loop(parts, sweep, (zero, zero, zero, zero))
    wall = KERNEL_WEIGHTS[0] * jnp.sum(down0 + ratio * down1, axis=0, keepdims=True)

    def combine(part, carry):
        rows_here = pl.ds(part * rows, rows)
        net = jnp.sum(up_ref[rows_here] - down_ref[rows_here], axis=1)
        net_ref[pl.ds(pl.multiple_of(part * rows + rows, rows), rows), :] = net
        return carry

    loop(parts, combine, 0)
    net_ref[rows - 1 : rows, :] = net_ref[rows : rows + 1, :]
    net_ref[rows + count : rows + count + 1, :] = net_ref[rows + count - 1 : rows + count, :]
    scale = KERNEL_WEIGHTS[0] * count / 2.0
    for part in range(parts):
        first = part * rows + rows
        heat_ref[part] = (net_ref[first - 1 : first - 1 + rows, :] - net_ref[first + 1 : first + 1 + rows, :]) * scale
    return wall


def arrive_kernel(slots, block_ref, cross_ref, share_ref, *refs):
    step_ref, emit_ref, decay_ref, outer_ref, inner_ref = refs[-5:]
    rows, cols = block_ref.shape[-2:]
    lane = lanes((rows, cols))
    me = lax.axis_index("wall")
    odd = lax.rem(lax.axis_index("azim"), 2) == 1

    def take(block, slot):
        absorb(block, (me ^ slot) * rows, rows, cross_ref, share_ref, step_ref, emit_ref, decay_ref)
        last, first = edge_tiles(block, lane)
        outer_ref[slot] = jnp.where(odd, last, first)
        inner_ref[slot] = jnp.where(odd, first, last)

    if len(block_ref.shape) == 3:
        take(block_ref, slot_here(slots))
    else:

        def body(i, carry):
            take(block_ref.at[i], i)
            return carry

        loop(block_ref.shape[0], body, 0)
    if slots[0] == 0:
        own = block_ref if len(block_ref.shape) == 3 else block_ref.at[0]
        edges = spread(own[COURANT], lane, PACKED, (1, 2, 4))
        for ref in (outer_ref, inner_ref):
            ref[0] = jnp.where(lane < PACKED, ref[0], edges)


def first_kernel(step_ref, emit_ref, decay_ref, outer_in_ref, inner_in_ref, heating_ref, wall_ref, outer_ref, inner_ref, *scratch):
    heat_ref = scratch[-1]
    parts, rows, cols = heating_ref.shape
    me = lax.axis_index("wall")
    wall_ref[...] = radiate(rows, step_ref, emit_ref, decay_ref, *scratch)
    lane = lanes((rows, cols))
    for s in range(parts):
        heating_ref[s] = heat_ref[me ^ s]
    for s in range(1, parts):
        outer_ref[s] = outer_in_ref[s]
        inner_ref[s] = inner_in_ref[s]
    here = (lane >= HEAT_AT) & (lane < HEAT_AT + EDGE)
    edges = roll(heat_ref[me], EDGE // 2 + HEAT_AT)
    outer_ref[0] = jnp.where(here, edges, outer_in_ref[0])
    inner_ref[0] = jnp.where(here, edges, inner_in_ref[0])


def coefficients(courant):
    return (0.3 - 0.75 * courant, 0.3 + 0.75 * courant, 0.15 * courant - 0.12, -0.12 - 0.15 * courant, 0.02 - courant / 60.0, 0.02 + courant / 60.0)


def stencil(value, halo, factors, lane, cols):
    total = 0.6 * value
    for offset, factor in zip(OFFSETS, factors):
        if halo is None:
            source = value
        elif offset > 0:
            source = jnp.where(lane < offset, halo, value)
        else:
            source = jnp.where(lane >= cols + offset, halo, value)
        total = total + factor * roll(source, -offset)
    return total


def center_kernel(ids, *refs):
    blocks = refs[: len(ids)]
    heating_ref, middle_ref, packed_ref = refs[len(ids) :]
    rows, cols = heating_ref.shape[1:]
    lane = lanes((rows, cols))

    def advance(block, s):
        factors = coefficients(block[COURANT])
        packed_ref[s] = spread(block[COURANT], lane, 0, (1, 2, 4, 8))
        for k in range(COMPS):
            moved = stencil(block[k], None, factors, lane, cols)
            if k == 0:
                moved = moved + COUPLING * heating_ref[s]
            middle_ref[s, k] = moved

    if len(ids) > 1:
        for block, slot in zip(blocks, ids):
            advance(block, slot_here(slot))
    else:

        def body(s, carry):
            advance(blocks[0].at[s], s)
            return carry

        loop(heating_ref.shape[0], body, 0)


def border_kernel(middle_in_ref, packed_ref, my_outer_ref, my_inner_ref, outer_ref, inner_ref, middle_ref, edge_ref, change_ref):
    parts, comps, rows, cols = middle_ref.shape
    lane = lanes((rows, cols))
    at = lax.rem(lane, EDGE)
    three = EDGE // 2
    odd = lax.rem(lax.axis_index("azim"), 2) == 1

    def sides(s):
        outer, inner = outer_ref[s], inner_ref[s]
        my_outer, my_inner = my_outer_ref[s], my_inner_ref[s]
        return (
            jnp.where(odd, inner, outer), jnp.where(odd, outer, inner),
            jnp.where(odd, my_outer, my_inner), jnp.where(odd, my_inner, my_outer),
        )

    def differ(s, carry):
        left, right, last, first = sides(s)
        left, right = left - last, right - first
        factors = coefficients(packed_ref[s])
        change = jnp.zeros((rows, cols), jnp.float32)
        for reach in range(1, three + 1):
            ahead = factors[2 * reach - 2] * roll(right, three - reach)
            behind = factors[2 * reach - 1] * roll(left, reach - three)
            ahead = jnp.where((at >= three - reach) & (at < three), ahead, 0.0)
            change = change + jnp.where((at >= three) & (at < three + reach), behind, ahead)
        change_ref[s] = change
        return carry

    loop(parts, differ, 0)

    left, right, last, first = sides(0)
    outside = jnp.where(at < three, left, right)
    courant = jnp.where(lane < 8 * EDGE, roll(outside, -PACKED), roll(outside, 8 * EDGE - PACKED))
    factors = dict(zip(OFFSETS, coefficients(courant)))
    factors[0] = 0.6
    edge = jnp.where(lane < EDGE, COUPLING * roll(outside, -HEAT_AT), 0.0)
    for offset in range(-three, three + 1):
        behind = roll(jnp.where(at <= EDGE - 1 + offset, left, last), -(three + offset))
        ahead = roll(jnp.where(at < offset, first, right), three - offset)
        edge = edge + factors[offset] * jnp.where(at <= three - 1 - offset, behind, ahead)
    edge_change = edge

    border = (lane < three) | (lane >= cols - three)

    def mend(s, carry):
        change = change_ref[s]
        for k in range(COMPS):
            middle_ref[s, k] = middle_in_ref[s, k] + jnp.where(border, roll(change, -(EDGE * k + three)), 0.0)
        return carry

    loop(parts, mend, 0)
    edge = edge_change
    for k in range(COMPS):
        edge_ref[k] = roll(edge, -(EDGE * k + three))


def last_kernel(block_ref, middle_ref, edge_ref, wall_in_ref, cross_ref, share_ref, out_ref, wall_ref, *scratch):
    heat_ref = scratch[-1]
    own = block_ref if len(block_ref.shape) == 3 else block_ref.at[0]
    rows, cols = out_ref.shape[1:]
    lane = lanes((rows, cols))
    me = lax.axis_index("wall")
    step_ref, emit_ref, decay_ref = scratch[:3]

    def take(slot, carry):
        absorb(middle_ref.at[slot], (me ^ slot) * rows, rows, cross_ref, share_ref, step_ref, emit_ref, decay_ref)
        return carry

    loop(middle_ref.shape[0], take, 0)
    wall = radiate(rows, *scratch)
    wall_ref[...] = 0.5 * (wall_in_ref[...] + wall)
    factors = coefficients(own[COURANT])
    for k in range(COMPS):
        moved = stencil(middle_ref[0, k], edge_ref[k], factors, lane, cols)
        if k == 0:
            moved = moved + COUPLING * heat_ref[me]
        out_ref[k] = 0.5 * (own[k] + moved)


def band_tables(absorb_index, band_index, cross_sections, band_fractions, height, cols):
    entries = cross_sections.shape[0]
    table_slots = lax.broadcasted_iota(jnp.int32, (1, 1, entries), 2)
    area = jnp.sum(jnp.where(absorb_index[:, :, None] == table_slots, cross_sections[None, None, :], 0.0), axis=2)
    share = jnp.sum(jnp.where(band_index[:, None] == table_slots[0], band_fractions[None, :], 0.0), axis=1)
    area = jnp.broadcast_to((area * height)[:, :, None], area.shape + (cols,))
    return area, jnp.broadcast_to(share[:, None], share.shape + (cols,))


def exchange(x, axis, distance):
    return lax.ppermute(x, axis, [(i, i ^ distance) for i in range(lax.axis_size(axis))])


EXCHANGES = ((1, 2, 3, 0), (2, 3, 0, 1), (3, 0, 1, 2))


def copy_kernel(source_ref, *refs):
    for ref in refs:
        ref[...] = source_ref[...]


def gather_lines(block):
    count = lax.axis_size("wall")
    if count == 4:
        blocks, slots = [block], [(0,) * count]
        copies = list(call(copy_kernel, [block.shape] * 2, [], block))
        for targets in EXCHANGES:
            sent = copies.pop() if copies and targets != EXCHANGES[0] else block
            blocks.append(lax.ppermute(sent, "wall", list(enumerate(targets))))
            slots.append(tuple(w ^ targets.index(w) for w in range(count)))
        return blocks, tuple(slots)
    stack = block[None]
    for step in range(count.bit_length() - 1):
        stack = jnp.concatenate([stack, exchange(stack, "wall", 1 << step)])
    return [stack], ((0,) * count,)


def slot_here(slots):
    me = lax.axis_index("wall")
    if len(set(slots)) == 1:
        return slots[0]
    return sum(jnp.where(me == w, slot, 0) for w, slot in enumerate(slots))


VMEM = pl.BlockSpec(memory_space=pltpu.VMEM)


def call(kernel, outs, scratch, *args, aliases=None, limit=32 * 1024 * 1024):
    return pl.pallas_call(
        kernel,
        out_shape=[jax.ShapeDtypeStruct(shape, jnp.float32) for shape in outs],
        in_specs=[VMEM] * len(args),
        out_specs=[VMEM] * len(outs),
        scratch_shapes=[pltpu.VMEM(shape, jnp.float32) for shape in scratch],
        input_output_aliases=aliases or {},
        compiler_params=pltpu.CompilerParams(vmem_limit_bytes=limit),
    )(*args)


def join_kernel(state_ref, courant_ref, block_ref, sems):
    copies = [pltpu.make_async_copy(courant_ref, block_ref.at[COURANT], sems.at[PIECES])]
    for i in range(PIECES):
        piece = pl.ds(i * (COMPS // PIECES), COMPS // PIECES)
        copies.append(pltpu.make_async_copy(state_ref.at[piece], block_ref.at[piece], sems.at[i]))
    for copy in copies:
        copy.start()
    for copy in copies:
        copy.wait()


def local(state, courant, cross_sections, band_fractions, absorb_index, band_index):
    comps, stations, rows, cols = state.shape
    parts = lax.axis_size("wall")
    count = parts * rows
    ring = lax.axis_size("azim")
    tile = (rows, cols)
    block = pl.pallas_call(
        join_kernel,
        out_shape=pltpu.VMEM((TILES,) + tile, jnp.float32),
        in_specs=[pl.BlockSpec(memory_space=pl.ANY)] * 2,
        out_specs=VMEM,
        scratch_shapes=[pltpu.SemaphoreType.DMA((PIECES + 1,))],
        compiler_params=pltpu.CompilerParams(vmem_limit_bytes=60 * 1024 * 1024),
    )(state.reshape(comps, rows, cols), courant.reshape(tile))
    cross, share = band_tables(absorb_index, band_index, cross_sections, band_fractions, 1.0 / count, cols)
    blocks, ids = gather_lines(block)
    deep = (count, BANDS, cols)
    flat = (count, BANDS // 2, cols)
    whole = (parts,) + tile
    message = (parts,) + tile
    ends = (parts, 2, BANDS, cols)
    both = (2,) + deep
    state_of = [ends, deep, both, message, message]
    held = []
    for received, slot in zip(blocks, ids):
        held = call(
            functools.partial(arrive_kernel, slot), state_of, [], received, cross, share, *held,
            aliases={3 + j: j for j in range(len(held))},
        )
    scratch = [flat, flat, (count + 2 * rows, cols), whole]
    heating, wall, my_outer, my_inner = call(first_kernel, [whole, (1, cols), message, message], scratch, *held)
    inner = lax.ppermute(my_inner, "azim", [(i, i ^ 1) for i in range(ring)])
    outer = lax.ppermute(my_outer, "azim", [(i, (i + 1) % ring if i % 2 else (i - 1) % ring) for i in range(ring)])
    middle, packed = call(
        functools.partial(center_kernel, ids), [(parts, comps) + tile, whole], [], *blocks, heating,
    )
    middle, edge = call(
        border_kernel, [(parts, comps) + tile, (comps,) + tile], [message],
        middle, packed, my_outer, my_inner, outer, inner, aliases={0: 0},
    )
    new_state, wall = call(
        last_kernel, [(comps,) + tile, (1, cols)], [ends, deep, both] + scratch,
        blocks[0], middle, edge, wall, cross, share,
    )
    return new_state.reshape(state.shape), wall


def solution(mesh):
    return jax.shard_map(
        local,
        mesh=mesh,
        in_specs=(P(None, "case", "wall", "azim"), P("case", "wall", "azim"), P(), P(), P(), P()),
        out_specs=(P(None, "case", "wall", "azim"), P("case", "azim")),
        check_vma=False,
    )
```

```python
import functools

import jax
import jax.numpy as jnp
from jax import lax
from jax.experimental import pallas as pl
from jax.experimental.pallas import tpu as pltpu
from jax.sharding import PartitionSpec as P

KERNEL_WEIGHTS = (0.55, 0.45)
KERNEL_RATES = (1.15, 3.4)
COUPLING = 0.1
LOG2E = 1.4426950408889634
COMPS = 12
SPECIES = 11
BANDS = 16
EDGE = 6
HALF = 3
SHARE = 3
COURANT = 12
PIECES = 3
TILES = 13
PACKED = EDGE * COMPS
HEAT_AT = PACKED + 8 * EDGE
OFFSETS = (1, -1, 2, -2, 3, -3)


def lanes(shape):
    return lax.broadcasted_iota(jnp.int32, shape, len(shape) - 1)


def roll(x, shift):
    return pltpu.roll(x, shift % x.shape[-1], x.ndim - 1)


def pack_kernel(state_ref, courant_ref, block_ref, sems):
    copies = [pltpu.make_async_copy(courant_ref, block_ref.at[COURANT], sems.at[PIECES])]
    for i in range(PIECES):
        piece = pl.ds(i * (COMPS // PIECES), COMPS // PIECES)
        copies.append(pltpu.make_async_copy(state_ref.at[piece], block_ref.at[piece], sems.at[i]))
    for copy in copies:
        copy.start()
    for copy in copies:
        copy.wait()


def edge_tiles(block, lane):
    cols = lane.shape[-1]
    last = jnp.zeros(lane.shape, jnp.float32)
    first = jnp.zeros(lane.shape, jnp.float32)
    for k in range(COMPS):
        here = (lane >= EDGE * k) & (lane < EDGE * (k + 1))
        last = jnp.where(here, roll(block[k], EDGE * k - (cols - EDGE)), last)
        first = jnp.where(here, roll(block[k], EDGE * k), first)
    return last, first


def border_tiles(block, lane, start):
    cols = lane.shape[-1]
    last = jnp.zeros(lane.shape, jnp.float32)
    first = jnp.zeros(lane.shape, jnp.float32)
    for k in range(COMPS):
        left = start + HALF * k
        here = (lane >= left) & (lane < left + HALF)
        last = jnp.where(here, roll(block[k], left - (cols - HALF)), last)
        first = jnp.where(here, roll(block[k], left), first)
    return last, first


def repeat(group, width):
    group = group + roll(group, width)
    group = group + roll(group, 2 * width)
    return group + roll(group, 4 * width) + roll(group, 8 * width)


def spread(value, lane, start, widths):
    group = jnp.where((lane >= start) & (lane < start + EDGE), roll(value, EDGE // 2 + start), 0.0)
    for width in widths:
        group = group + roll(group, EDGE * width)
    return group


def loop(count, body, carry):
    if count <= 4:
        for i in range(count):
            carry = body(i, carry)
        return carry
    return lax.fori_loop(0, count, body, carry)


def decay(gap, decay_ref, at):
    for i, rate in enumerate(KERNEL_RATES):
        decay_ref[i, at] = jnp.exp2(gap * (-0.5 * LOG2E * rate))


def absorb(block, base, rows, cross_ref, share_ref, step_ref, emit_ref, decay_ref):
    hot = block[0]
    hot = hot * hot
    hot = hot * hot
    before = None
    for r in range(rows):
        step = None
        for k in range(SPECIES):
            term = cross_ref[k] * block[1 + k, pl.ds(r, 1), :]
            step = term if step is None else step + term
        if r in (0, rows - 1):
            step_ref[base // rows, min(r, 1)] = step
        emit_ref[base + r] = share_ref[...] * step * hot[r : r + 1]
        if r:
            decay(before + step, decay_ref, base + r)
        before = step


def radiate(rows, step_ref, emit_ref, decay_ref, up_ref, down_ref, net_ref, heat_ref):
    count = emit_ref.shape[0]
    parts = count // rows
    cols = emit_ref.shape[-1]

    zero = jnp.zeros((BANDS, cols), jnp.float32)

    def attenuate(part, before):
        decay(before + step_ref[part, 0], decay_ref, part * rows)
        return step_ref[part, 1]

    loop(parts, attenuate, zero)

    ratio = KERNEL_WEIGHTS[1] / KERNEL_WEIGHTS[0]

    def halve(x):
        return x[: BANDS // 2] + x[BANDS // 2 :]

    def sweep(part, carry):
        up0, up1, down0, down1 = carry
        for r in range(rows):
            at = part * rows + r
            emitted = emit_ref[at]
            up0 = up0 * decay_ref[0, at] + emitted
            up1 = up1 * decay_ref[1, at] + emitted
            up_ref[at] = halve(up0 + ratio * up1)
            back = count - 1 - at
            emitted = emit_ref[back]
            down0 = down0 + emitted
            down1 = down1 + emitted
            down_ref[back] = halve(down0 + ratio * down1)
            down0 = down0 * decay_ref[0, back]
            down1 = down1 * decay_ref[1, back]
        return up0, up1, down0, down1

    _, _, down0, down1 = loop(parts, sweep, (zero, zero, zero, zero))
    wall = KERNEL_WEIGHTS[0] * jnp.sum(down0 + ratio * down1, axis=0, keepdims=True)

    def combine(part, carry):
        rows_here = pl.ds(part * rows, rows)
        net = jnp.sum(up_ref[rows_here] - down_ref[rows_here], axis=1)
        net_ref[pl.ds(pl.multiple_of(part * rows + rows, rows), rows), :] = net
        return carry

    loop(parts, combine, 0)
    net_ref[rows - 1 : rows, :] = net_ref[rows : rows + 1, :]
    net_ref[rows + count : rows + count + 1, :] = net_ref[rows + count - 1 : rows + count, :]
    scale = KERNEL_WEIGHTS[0] * count / 2.0
    for part in range(parts):
        first = part * rows + rows
        heat_ref[part] = (net_ref[first - 1 : first - 1 + rows, :] - net_ref[first + 1 : first + 1 + rows, :]) * scale
    return wall


def seat(arrival):
    return (0, 0) if arrival == 0 else (1 + (arrival - 1) // SHARE, (arrival - 1) % SHARE * HALF * COMPS)


def arrive_kernel(arrival, slots, block_ref, cross_ref, share_ref, *refs):
    step_ref, emit_ref, decay_ref, outer_ref, inner_ref = refs[-5:]
    rows, cols = block_ref.shape[-2:]
    lane = lanes((rows, cols))
    me = lax.axis_index("wall")
    odd = lax.rem(lax.axis_index("azim"), 2) == 1

    def take(block, slot):
        absorb(block, (me ^ slot) * rows, rows, cross_ref, share_ref, step_ref, emit_ref, decay_ref)

    def pack(block, arrival):
        tile, start = seat(arrival)
        last, first = edge_tiles(block, lane) if arrival == 0 else border_tiles(block, lane, start)
        for ref, value in ((outer_ref, jnp.where(odd, last, first)), (inner_ref, jnp.where(odd, first, last))):
            ref[tile] = value if start == 0 else jnp.where(lane < start, ref[tile], value)

    if len(block_ref.shape) == 3:
        take(block_ref, slot_here(slots))
        pack(block_ref, arrival)
    else:

        def body(i, carry):
            take(block_ref.at[i], i)
            return carry

        loop(block_ref.shape[0], body, 0)
        for i in range(block_ref.shape[0]):
            pack(block_ref.at[i], i)
    if slots[0] == 0:
        own = block_ref if len(block_ref.shape) == 3 else block_ref.at[0]
        edges = spread(own[COURANT], lane, PACKED, (1, 2, 4))
        for ref in (outer_ref, inner_ref):
            ref[0] = jnp.where(lane < PACKED, ref[0], edges)


def first_kernel(step_ref, emit_ref, decay_ref, outer_in_ref, inner_in_ref, heating_ref, wall_ref, outer_ref, inner_ref, *scratch):
    heat_ref = scratch[-1]
    parts, rows, cols = heating_ref.shape
    me = lax.axis_index("wall")
    wall_ref[...] = radiate(rows, step_ref, emit_ref, decay_ref, *scratch)
    lane = lanes((rows, cols))
    for s in range(parts):
        heating_ref[s] = heat_ref[me ^ s]
    for s in range(1, outer_ref.shape[0]):
        outer_ref[s] = outer_in_ref[s]
        inner_ref[s] = inner_in_ref[s]
    here = (lane >= HEAT_AT) & (lane < HEAT_AT + EDGE)
    edges = roll(heat_ref[me], EDGE // 2 + HEAT_AT)
    outer_ref[0] = jnp.where(here, edges, outer_in_ref[0])
    inner_ref[0] = jnp.where(here, edges, inner_in_ref[0])


def coefficients(courant):
    return (0.3 - 0.75 * courant, 0.3 + 0.75 * courant, 0.15 * courant - 0.12, -0.12 - 0.15 * courant, 0.02 - courant / 60.0, 0.02 + courant / 60.0)


def stencil(value, halo, factors, lane, cols):
    total = 0.6 * value
    for offset, factor in zip(OFFSETS, factors):
        if halo is None:
            source = value
        elif offset > 0:
            source = jnp.where(lane < offset, halo, value)
        else:
            source = jnp.where(lane >= cols + offset, halo, value)
        total = total + factor * roll(source, -offset)
    return total


def center_kernel(ids, *refs):
    blocks = refs[: len(ids)]
    heating_ref, middle_ref, packed_ref = refs[len(ids) :]
    rows, cols = heating_ref.shape[1:]
    lane = lanes((rows, cols))

    def advance(block, s, slot):
        factors = coefficients(block[COURANT])
        for k in range(COMPS):
            moved = stencil(block[k], None, factors, lane, cols)
            if k == 0:
                moved = moved + COUPLING * heating_ref[slot]
            middle_ref[s, k] = moved

    if len(ids) > 1:
        for s, (block, slots) in enumerate(zip(blocks, ids)):
            advance(block, s, slot_here(slots))
        arrivals = blocks
    else:

        def body(s, carry):
            advance(blocks[0].at[s], s, s)
            return carry

        loop(heating_ref.shape[0], body, 0)
        arrivals = [blocks[0].at[s] for s in range(heating_ref.shape[0])]

    odd = lax.rem(lax.axis_index("azim"), 2) == 1
    packed_ref[...] = jnp.zeros(packed_ref.shape, jnp.float32)
    for arrival, block in enumerate(arrivals):
        courant = block[COURANT]
        tile, start = seat(arrival)
        if arrival == 0:
            own = repeat(jnp.where(lane < EDGE, roll(courant, HALF), 0.0), EDGE)
            packed_ref[0, 0] = own
            continue
        here = (lane >= start) & (lane < start + HALF)
        right = repeat(jnp.where(here, roll(courant, start + HALF), 0.0), HALF)
        left = repeat(jnp.where(here, roll(courant, start), 0.0), HALF)
        fresh = lane >= start
        packed_ref[0, tile] = jnp.where(fresh, right, packed_ref[0, tile])
        packed_ref[1, tile] = jnp.where(fresh, left, packed_ref[1, tile])


def border_kernel(middle_in_ref, packed_ref, my_outer_ref, my_inner_ref, outer_ref, inner_ref, middle_ref, edge_ref, change_ref):
    parts, comps, rows, cols = middle_ref.shape
    lane = lanes((rows, cols))
    at = lax.rem(lane, EDGE)
    three = EDGE // 2
    odd = lax.rem(lax.axis_index("azim"), 2) == 1

    def sides(s):
        outer, inner = outer_ref[s], inner_ref[s]
        my_outer, my_inner = my_outer_ref[s], my_inner_ref[s]
        return (
            jnp.where(odd, inner, outer), jnp.where(odd, outer, inner),
            jnp.where(odd, my_outer, my_inner), jnp.where(odd, my_inner, my_outer),
        )

    tiles = outer_ref.shape[0]
    left, right, last, first = sides(0)
    factors = coefficients(packed_ref[0, 0])
    far, near = right - first, left - last
    change = jnp.zeros((rows, cols), jnp.float32)
    for reach in range(1, three + 1):
        ahead = factors[2 * reach - 2] * roll(far, three - reach)
        behind = factors[2 * reach - 1] * roll(near, reach - three)
        ahead = jnp.where((at >= three - reach) & (at < three), ahead, 0.0)
        change = change + jnp.where((at >= three) & (at < three + reach), behind, ahead)
    change_ref[0, 0] = change
    third = lax.rem(lane, three)
    even_group = at < three
    for tile in range(1, tiles):
        other_left, other_right, other_last, other_first = sides(tile)
        far, near = other_right - other_first, other_left - other_last
        ahead_factors, behind_factors = coefficients(packed_ref[0, tile]), coefficients(packed_ref[1, tile])
        ahead = behind = jnp.zeros((rows, cols), jnp.float32)
        for reach in range(1, three + 1):
            term = ahead_factors[2 * reach - 2] * roll(far, three - reach)
            ahead = ahead + jnp.where(third >= three - reach, term, 0.0)
            term = behind_factors[2 * reach - 1] * roll(near, reach - three)
            behind = behind + jnp.where(third < reach, term, 0.0)
        behind = roll(behind, three)
        change_ref[0, tile] = jnp.where(even_group, ahead, behind)
        change_ref[1, tile] = jnp.where(even_group, behind, ahead)

    outside = jnp.where(at < three, left, right)
    courant = jnp.where(lane < 8 * EDGE, roll(outside, -PACKED), roll(outside, 8 * EDGE - PACKED))
    factors = dict(zip(OFFSETS, coefficients(courant)))
    factors[0] = 0.6
    edge = jnp.where(lane < EDGE, COUPLING * roll(outside, -HEAT_AT), 0.0)
    for offset in range(-three, three + 1):
        behind = roll(jnp.where(at <= EDGE - 1 + offset, left, last), -(three + offset))
        ahead = roll(jnp.where(at < offset, first, right), three - offset)
        edge = edge + factors[offset] * jnp.where(at <= three - 1 - offset, behind, ahead)
    edge_change = edge

    border = (lane < three) | (lane >= cols - three)
    for arrival in range(parts):
        tile, start = seat(arrival)
        changes = change_ref[0, tile], change_ref[1, tile]
        for k in range(COMPS):
            moved = changes[0] if arrival == 0 else changes[k % 2]
            width = EDGE if arrival == 0 else three
            gain = jnp.where(border, roll(moved, -(start + width * k + three)), 0.0)
            middle_ref[arrival, k] = middle_in_ref[arrival, k] + gain
    edge = edge_change
    for k in range(COMPS):
        edge_ref[k] = roll(edge, -(EDGE * k + three))


def last_kernel(ids, block_ref, middle_ref, edge_ref, wall_in_ref, cross_ref, share_ref, out_ref, wall_ref, *scratch):
    heat_ref = scratch[-1]
    own = block_ref if len(block_ref.shape) == 3 else block_ref.at[0]
    rows, cols = out_ref.shape[1:]
    lane = lanes((rows, cols))
    me = lax.axis_index("wall")
    step_ref, emit_ref, decay_ref = scratch[:3]

    def take(s, carry):
        slot = slot_here(ids[s]) if len(ids) > 1 else s
        absorb(middle_ref.at[s], (me ^ slot) * rows, rows, cross_ref, share_ref, step_ref, emit_ref, decay_ref)
        return carry

    loop(middle_ref.shape[0], take, 0)
    wall = radiate(rows, *scratch)
    wall_ref[...] = 0.5 * (wall_in_ref[...] + wall)
    factors = coefficients(own[COURANT])
    for k in range(COMPS):
        moved = stencil(middle_ref[0, k], edge_ref[k], factors, lane, cols)
        if k == 0:
            moved = moved + COUPLING * heat_ref[me]
        out_ref[k] = 0.5 * (own[k] + moved)


def band_tables(absorb_index, band_index, cross_sections, band_fractions, height, cols):
    entries = cross_sections.shape[0]
    table_slots = lax.broadcasted_iota(jnp.int32, (1, 1, entries), 2)
    area = jnp.sum(jnp.where(absorb_index[:, :, None] == table_slots, cross_sections[None, None, :], 0.0), axis=2)
    share = jnp.sum(jnp.where(band_index[:, None] == table_slots[0], band_fractions[None, :], 0.0), axis=1)
    area = jnp.broadcast_to((area * height)[:, :, None], area.shape + (cols,))
    return area, jnp.broadcast_to(share[:, None], share.shape + (cols,))


def exchange(x, axis, distance):
    return lax.ppermute(x, axis, [(i, i ^ distance) for i in range(lax.axis_size(axis))])


EXCHANGES = ((1, 2, 3, 0), (2, 3, 0, 1), (3, 0, 1, 2))


def copy_kernel(source_ref, *refs):
    for ref in refs:
        ref[...] = source_ref[...]


def gather_lines(block):
    count = lax.axis_size("wall")
    if count == 4:
        blocks, slots = [block], [(0,) * count]
        copies = list(call(copy_kernel, [block.shape] * 2, [], block))
        for targets in EXCHANGES:
            sent = copies.pop() if copies and targets != EXCHANGES[0] else block
            blocks.append(lax.ppermute(sent, "wall", list(enumerate(targets))))
            slots.append(tuple(w ^ targets.index(w) for w in range(count)))
        return blocks, tuple(slots)
    stack = block[None]
    for step in range(count.bit_length() - 1):
        stack = jnp.concatenate([stack, exchange(stack, "wall", 1 << step)])
    return [stack], ((0,) * count,)


def slot_here(slots):
    me = lax.axis_index("wall")
    if len(set(slots)) == 1:
        return slots[0]
    return sum(jnp.where(me == w, slot, 0) for w, slot in enumerate(slots))


VMEM = pl.BlockSpec(memory_space=pltpu.VMEM)


def call(kernel, outs, scratch, *args, aliases=None, limit=32 * 1024 * 1024):
    return pl.pallas_call(
        kernel,
        out_shape=[jax.ShapeDtypeStruct(shape, jnp.float32) for shape in outs],
        in_specs=[VMEM] * len(args),
        out_specs=[VMEM] * len(outs),
        scratch_shapes=[pltpu.VMEM(shape, jnp.float32) for shape in scratch],
        input_output_aliases=aliases or {},
        compiler_params=pltpu.CompilerParams(vmem_limit_bytes=limit),
    )(*args)


def join_kernel(state_ref, courant_ref, block_ref, sems):
    copies = [pltpu.make_async_copy(courant_ref, block_ref.at[COURANT], sems.at[PIECES])]
    for i in range(PIECES):
        piece = pl.ds(i * (COMPS // PIECES), COMPS // PIECES)
        copies.append(pltpu.make_async_copy(state_ref.at[piece], block_ref.at[piece], sems.at[i]))
    for copy in copies:
        copy.start()
    for copy in copies:
        copy.wait()


def local(state, courant, cross_sections, band_fractions, absorb_index, band_index):
    comps, stations, rows, cols = state.shape
    parts = lax.axis_size("wall")
    count = parts * rows
    ring = lax.axis_size("azim")
    tile = (rows, cols)
    block = pl.pallas_call(
        join_kernel,
        out_shape=pltpu.VMEM((TILES,) + tile, jnp.float32),
        in_specs=[pl.BlockSpec(memory_space=pl.ANY)] * 2,
        out_specs=VMEM,
        scratch_shapes=[pltpu.SemaphoreType.DMA((PIECES + 1,))],
        compiler_params=pltpu.CompilerParams(vmem_limit_bytes=60 * 1024 * 1024),
    )(state.reshape(comps, rows, cols), courant.reshape(tile))
    cross, share = band_tables(absorb_index, band_index, cross_sections, band_fractions, 1.0 / count, cols)
    blocks, ids = gather_lines(block)
    deep = (count, BANDS, cols)
    flat = (count, BANDS // 2, cols)
    whole = (parts,) + tile
    message = (1 + pl.cdiv(parts - 1, SHARE),) + tile
    ends = (parts, 2, BANDS, cols)
    both = (2,) + deep
    state_of = [ends, deep, both, message, message]
    held = []
    for arrival, (received, slot) in enumerate(zip(blocks, ids)):
        held = call(
            functools.partial(arrive_kernel, arrival, slot), state_of, [], received, cross, share, *held,
            aliases={3 + j: j for j in range(len(held))},
        )
    scratch = [flat, flat, (count + 2 * rows, cols), whole]
    heating, wall, my_outer, my_inner = call(first_kernel, [whole, (1, cols), message, message], scratch, *held)
    inner = lax.ppermute(my_inner, "azim", [(i, i ^ 1) for i in range(ring)])
    outer = lax.ppermute(my_outer, "azim", [(i, (i + 1) % ring if i % 2 else (i - 1) % ring) for i in range(ring)])
    middle, packed = call(
        functools.partial(center_kernel, ids), [(parts, comps) + tile, (2,) + message], [], *blocks, heating,
    )
    middle, edge = call(
        border_kernel, [(parts, comps) + tile, (comps,) + tile], [(2,) + message],
        middle, packed, my_outer, my_inner, outer, inner, aliases={0: 0},
    )
    new_state, wall = call(
        functools.partial(last_kernel, ids), [(comps,) + tile, (1, cols)], [ends, deep, both] + scratch,
        blocks[0], middle, edge, wall, cross, share,
    )
    return new_state.reshape(state.shape), wall


def solution(mesh):
    return jax.shard_map(
        local,
        mesh=mesh,
        in_specs=(P(None, "case", "wall", "azim"), P("case", "wall", "azim"), P(), P(), P(), P()),
        out_specs=(P(None, "case", "wall", "azim"), P("case", "azim")),
        check_vma=False,
    )
```

```python
import functools

import jax
import jax.numpy as jnp
from jax import lax
from jax.experimental import pallas as pl
from jax.experimental.pallas import tpu as pltpu
from jax.sharding import PartitionSpec as P

KERNEL_WEIGHTS = (0.55, 0.45)
KERNEL_RATES = (1.15, 3.4)
COUPLING = 0.1
LOG2E = 1.4426950408889634
COMPS = 12
SPECIES = 11
BANDS = 16
EDGE = 6
HALF = 3
SHARE = 3
COURANT = 12
PIECES = 3
TILES = 13
PACKED = EDGE * COMPS
HEAT_AT = PACKED + 8 * EDGE
OFFSETS = (1, -1, 2, -2, 3, -3)


def lanes(shape):
    return lax.broadcasted_iota(jnp.int32, shape, len(shape) - 1)


def roll(x, shift):
    return pltpu.roll(x, shift % x.shape[-1], x.ndim - 1)


def pack_kernel(state_ref, courant_ref, block_ref, sems):
    copies = [pltpu.make_async_copy(courant_ref, block_ref.at[COURANT], sems.at[PIECES])]
    for i in range(PIECES):
        piece = pl.ds(i * (COMPS // PIECES), COMPS // PIECES)
        copies.append(pltpu.make_async_copy(state_ref.at[piece], block_ref.at[piece], sems.at[i]))
    for copy in copies:
        copy.start()
    for copy in copies:
        copy.wait()


def edge_tiles(block, lane):
    cols = lane.shape[-1]
    last = jnp.zeros(lane.shape, jnp.float32)
    first = jnp.zeros(lane.shape, jnp.float32)
    for k in range(COMPS):
        here = (lane >= EDGE * k) & (lane < EDGE * (k + 1))
        last = jnp.where(here, roll(block[k], EDGE * k - (cols - EDGE)), last)
        first = jnp.where(here, roll(block[k], EDGE * k), first)
    return last, first


def border_tiles(block, lane, start):
    cols = lane.shape[-1]
    last = jnp.zeros(lane.shape, jnp.float32)
    first = jnp.zeros(lane.shape, jnp.float32)
    for k in range(COMPS):
        left = start + HALF * k
        here = (lane >= left) & (lane < left + HALF)
        last = jnp.where(here, roll(block[k], left - (cols - HALF)), last)
        first = jnp.where(here, roll(block[k], left), first)
    return last, first


def repeat(group, width):
    group = group + roll(group, width)
    group = group + roll(group, 2 * width)
    return group + roll(group, 4 * width) + roll(group, 8 * width)


def spread(value, lane, start, widths):
    group = jnp.where((lane >= start) & (lane < start + EDGE), roll(value, EDGE // 2 + start), 0.0)
    for width in widths:
        group = group + roll(group, EDGE * width)
    return group


def loop(count, body, carry):
    if count <= 4:
        for i in range(count):
            carry = body(i, carry)
        return carry
    return lax.fori_loop(0, count, body, carry)


def decay(gap, decay_ref, at):
    for i, rate in enumerate(KERNEL_RATES):
        decay_ref[i, at] = jnp.exp2(gap * (-0.5 * LOG2E * rate))


def absorb(block, base, rows, cross_ref, share_ref, step_ref, emit_ref, decay_ref):
    hot = block[0]
    hot = hot * hot
    hot = hot * hot
    before = None
    for r in range(rows):
        step = None
        for k in range(SPECIES):
            term = cross_ref[k] * block[1 + k, pl.ds(r, 1), :]
            step = term if step is None else step + term
        if r in (0, rows - 1):
            step_ref[base // rows, min(r, 1)] = step
        emit_ref[base + r] = share_ref[...] * step * hot[r : r + 1]
        if r:
            decay(before + step, decay_ref, base + r)
        before = step


def radiate(rows, step_ref, emit_ref, decay_ref, up_ref, down_ref, net_ref, heat_ref):
    count = emit_ref.shape[0]
    parts = count // rows
    cols = emit_ref.shape[-1]

    zero = jnp.zeros((BANDS, cols), jnp.float32)

    def attenuate(part, before):
        decay(before + step_ref[part, 0], decay_ref, part * rows)
        return step_ref[part, 1]

    loop(parts, attenuate, zero)

    ratio = KERNEL_WEIGHTS[1] / KERNEL_WEIGHTS[0]

    def halve(x):
        return x[: BANDS // 2] + x[BANDS // 2 :]

    def sweep(part, carry):
        up0, up1, down0, down1 = carry
        for r in range(rows):
            at = part * rows + r
            emitted = emit_ref[at]
            up0 = up0 * decay_ref[0, at] + emitted
            up1 = up1 * decay_ref[1, at] + ratio * emitted
            up_ref[at] = halve(up0 + up1)
            back = count - 1 - at
            emitted = emit_ref[back]
            down0 = down0 + emitted
            down1 = down1 + ratio * emitted
            down_ref[back] = halve(down0 + down1)
            down0 = down0 * decay_ref[0, back]
            down1 = down1 * decay_ref[1, back]
        return up0, up1, down0, down1

    _, _, down0, down1 = loop(parts, sweep, (zero, zero, zero, zero))
    wall = KERNEL_WEIGHTS[0] * jnp.sum(down0 + down1, axis=0, keepdims=True)

    def combine(part, carry):
        rows_here = pl.ds(part * rows, rows)
        net = jnp.sum(up_ref[rows_here] - down_ref[rows_here], axis=1)
        net_ref[pl.ds(pl.multiple_of(part * rows + rows, rows), rows), :] = net
        return carry

    loop(parts, combine, 0)
    net_ref[rows - 1 : rows, :] = net_ref[rows : rows + 1, :]
    net_ref[rows + count : rows + count + 1, :] = net_ref[rows + count - 1 : rows + count, :]
    scale = KERNEL_WEIGHTS[0] * count / 2.0
    for part in range(parts):
        first = part * rows + rows
        heat_ref[part] = (net_ref[first - 1 : first - 1 + rows, :] - net_ref[first + 1 : first + 1 + rows, :]) * scale
    return wall


def seat(arrival):
    return (0, 0) if arrival == 0 else (1 + (arrival - 1) // SHARE, (arrival - 1) % SHARE * HALF * COMPS)


def arrive_kernel(arrival, slots, block_ref, cross_ref, share_ref, *refs):
    step_ref, emit_ref, decay_ref, outer_ref, inner_ref = refs[-5:]
    rows, cols = block_ref.shape[-2:]
    lane = lanes((rows, cols))
    me = lax.axis_index("wall")
    odd = lax.rem(lax.axis_index("azim"), 2) == 1

    def take(block, slot):
        absorb(block, (me ^ slot) * rows, rows, cross_ref, share_ref, step_ref, emit_ref, decay_ref)

    def pack(block, arrival):
        tile, start = seat(arrival)
        last, first = edge_tiles(block, lane) if arrival == 0 else border_tiles(block, lane, start)
        for ref, value in ((outer_ref, jnp.where(odd, last, first)), (inner_ref, jnp.where(odd, first, last))):
            ref[tile] = value if start == 0 else jnp.where(lane < start, ref[tile], value)

    if len(block_ref.shape) == 3:
        take(block_ref, slot_here(slots))
        pack(block_ref, arrival)
    else:

        def body(i, carry):
            take(block_ref.at[i], i)
            return carry

        loop(block_ref.shape[0], body, 0)
        for i in range(block_ref.shape[0]):
            pack(block_ref.at[i], i)
    if slots[0] == 0:
        own = block_ref if len(block_ref.shape) == 3 else block_ref.at[0]
        edges = spread(own[COURANT], lane, PACKED, (1, 2, 4))
        for ref in (outer_ref, inner_ref):
            ref[0] = jnp.where(lane < PACKED, ref[0], edges)


def first_kernel(step_ref, emit_ref, decay_ref, outer_in_ref, inner_in_ref, outer_ref, inner_ref, heating_ref, wall_ref, *scratch):
    heat_ref = scratch[-1]
    parts, rows, cols = heating_ref.shape
    me = lax.axis_index("wall")
    wall_ref[...] = radiate(rows, step_ref, emit_ref, decay_ref, *scratch)
    lane = lanes((rows, cols))
    for s in range(parts):
        heating_ref[s] = heat_ref[me ^ s]
    here = (lane >= HEAT_AT) & (lane < HEAT_AT + EDGE)
    edges = roll(heat_ref[me], EDGE // 2 + HEAT_AT)
    outer_ref[0] = jnp.where(here, edges, outer_in_ref[0])
    inner_ref[0] = jnp.where(here, edges, inner_in_ref[0])


def coefficients(courant):
    return (0.3 - 0.75 * courant, 0.3 + 0.75 * courant, 0.15 * courant - 0.12, -0.12 - 0.15 * courant, 0.02 - courant / 60.0, 0.02 + courant / 60.0)


def stencil(value, halo, factors, lane, cols):
    total = 0.6 * value
    for offset, factor in zip(OFFSETS, factors):
        if halo is None:
            source = value
        elif offset > 0:
            source = jnp.where(lane < offset, halo, value)
        else:
            source = jnp.where(lane >= cols + offset, halo, value)
        total = total + factor * roll(source, -offset)
    return total


def center_kernel(ids, *refs):
    blocks = refs[: len(ids)]
    heating_ref, middle_ref, packed_ref = refs[len(ids) :]
    rows, cols = heating_ref.shape[1:]
    lane = lanes((rows, cols))

    def advance(block, s, slot):
        factors = coefficients(block[COURANT])
        for k in range(COMPS):
            moved = stencil(block[k], None, factors, lane, cols)
            if k == 0:
                moved = moved + COUPLING * heating_ref[slot]
            middle_ref[s, k] = moved

    if len(ids) > 1:
        for s, (block, slots) in enumerate(zip(blocks, ids)):
            advance(block, s, slot_here(slots))
        arrivals = blocks
    else:

        def body(s, carry):
            advance(blocks[0].at[s], s, s)
            return carry

        loop(heating_ref.shape[0], body, 0)
        arrivals = [blocks[0].at[s] for s in range(heating_ref.shape[0])]

    odd = lax.rem(lax.axis_index("azim"), 2) == 1
    packed_ref[...] = jnp.zeros(packed_ref.shape, jnp.float32)
    for arrival, block in enumerate(arrivals):
        courant = block[COURANT]
        tile, start = seat(arrival)
        if arrival == 0:
            own = repeat(jnp.where(lane < EDGE, roll(courant, HALF), 0.0), EDGE)
            packed_ref[0, 0] = own
            continue
        here = (lane >= start) & (lane < start + HALF)
        right = repeat(jnp.where(here, roll(courant, start + HALF), 0.0), HALF)
        left = repeat(jnp.where(here, roll(courant, start), 0.0), HALF)
        fresh = lane >= start
        packed_ref[0, tile] = jnp.where(fresh, right, packed_ref[0, tile])
        packed_ref[1, tile] = jnp.where(fresh, left, packed_ref[1, tile])


def border_kernel(middle_in_ref, packed_ref, my_outer_ref, my_inner_ref, outer_ref, inner_ref, middle_ref, edge_ref, change_ref):
    parts, comps, rows, cols = middle_ref.shape
    lane = lanes((rows, cols))
    at = lax.rem(lane, EDGE)
    three = EDGE // 2
    odd = lax.rem(lax.axis_index("azim"), 2) == 1

    def sides(s):
        outer, inner = outer_ref[s], inner_ref[s]
        my_outer, my_inner = my_outer_ref[s], my_inner_ref[s]
        return (
            jnp.where(odd, inner, outer), jnp.where(odd, outer, inner),
            jnp.where(odd, my_outer, my_inner), jnp.where(odd, my_inner, my_outer),
        )

    tiles = outer_ref.shape[0]
    left, right, last, first = sides(0)
    factors = coefficients(packed_ref[0, 0])
    far, near = right - first, left - last
    change = jnp.zeros((rows, cols), jnp.float32)
    for reach in range(1, three + 1):
        ahead = factors[2 * reach - 2] * roll(far, three - reach)
        behind = factors[2 * reach - 1] * roll(near, reach - three)
        ahead = jnp.where((at >= three - reach) & (at < three), ahead, 0.0)
        change = change + jnp.where((at >= three) & (at < three + reach), behind, ahead)
    change_ref[0, 0] = change
    third = lax.rem(lane, three)
    even_group = at < three
    for tile in range(1, tiles):
        other_left, other_right, other_last, other_first = sides(tile)
        far, near = other_right - other_first, other_left - other_last
        ahead_factors, behind_factors = coefficients(packed_ref[0, tile]), coefficients(packed_ref[1, tile])
        ahead = behind = jnp.zeros((rows, cols), jnp.float32)
        for reach in range(1, three + 1):
            term = ahead_factors[2 * reach - 2] * roll(far, three - reach)
            ahead = ahead + jnp.where(third >= three - reach, term, 0.0)
            term = behind_factors[2 * reach - 1] * roll(near, reach - three)
            behind = behind + jnp.where(third < reach, term, 0.0)
        behind = roll(behind, three)
        change_ref[0, tile] = jnp.where(even_group, ahead, behind)
        change_ref[1, tile] = jnp.where(even_group, behind, ahead)

    outside = jnp.where(at < three, left, right)
    courant = jnp.where(lane < 8 * EDGE, roll(outside, -PACKED), roll(outside, 8 * EDGE - PACKED))
    factors = dict(zip(OFFSETS, coefficients(courant)))
    factors[0] = 0.6
    edge = jnp.where(lane < EDGE, COUPLING * roll(outside, -HEAT_AT), 0.0)
    for offset in range(-three, three + 1):
        behind = roll(jnp.where(at <= EDGE - 1 + offset, left, last), -(three + offset))
        ahead = roll(jnp.where(at < offset, first, right), three - offset)
        edge = edge + factors[offset] * jnp.where(at <= three - 1 - offset, behind, ahead)
    edge_change = edge

    border = (lane < three) | (lane >= cols - three)
    for arrival in range(parts):
        tile, start = seat(arrival)
        changes = change_ref[0, tile], change_ref[1, tile]
        for k in range(COMPS):
            moved = changes[0] if arrival == 0 else changes[k % 2]
            width = EDGE if arrival == 0 else three
            gain = jnp.where(border, roll(moved, -(start + width * k + three)), 0.0)
            middle_ref[arrival, k] = middle_in_ref[arrival, k] + gain
    edge = edge_change
    for k in range(COMPS):
        edge_ref[k] = roll(edge, -(EDGE * k + three))


def last_kernel(ids, block_ref, middle_ref, edge_ref, wall_in_ref, cross_ref, share_ref, out_ref, wall_ref, *scratch):
    heat_ref = scratch[-1]
    own = block_ref if len(block_ref.shape) == 3 else block_ref.at[0]
    rows, cols = out_ref.shape[1:]
    lane = lanes((rows, cols))
    me = lax.axis_index("wall")
    step_ref, emit_ref, decay_ref = scratch[:3]

    def take(s, carry):
        slot = slot_here(ids[s]) if len(ids) > 1 else s
        absorb(middle_ref.at[s], (me ^ slot) * rows, rows, cross_ref, share_ref, step_ref, emit_ref, decay_ref)
        return carry

    loop(middle_ref.shape[0], take, 0)
    wall = radiate(rows, *scratch)
    wall_ref[...] = 0.5 * (wall_in_ref[...] + wall)
    factors = coefficients(own[COURANT])
    for k in range(COMPS):
        moved = stencil(middle_ref[0, k], edge_ref[k], factors, lane, cols)
        if k == 0:
            moved = moved + COUPLING * heat_ref[me]
        out_ref[k] = 0.5 * (own[k] + moved)


def band_tables(absorb_index, band_index, cross_sections, band_fractions, height, cols):
    entries = cross_sections.shape[0]
    table_slots = lax.broadcasted_iota(jnp.int32, (1, 1, entries), 2)
    area = jnp.sum(jnp.where(absorb_index[:, :, None] == table_slots, cross_sections[None, None, :], 0.0), axis=2)
    share = jnp.sum(jnp.where(band_index[:, None] == table_slots[0], band_fractions[None, :], 0.0), axis=1)
    area = jnp.broadcast_to((area * height)[:, :, None], area.shape + (cols,))
    return area, jnp.broadcast_to(share[:, None], share.shape + (cols,))


def exchange(x, axis, distance):
    return lax.ppermute(x, axis, [(i, i ^ distance) for i in range(lax.axis_size(axis))])


EXCHANGES = ((1, 2, 3, 0), (2, 3, 0, 1), (3, 0, 1, 2))


def copy_kernel(source_ref, *refs):
    for ref in refs:
        ref[...] = source_ref[...]


def gather_lines(block):
    count = lax.axis_size("wall")
    if count == 4:
        blocks, slots = [block], [(0,) * count]
        copies = list(call(copy_kernel, [block.shape] * 2, [], block))
        for targets in EXCHANGES:
            sent = copies.pop() if copies and targets != EXCHANGES[0] else block
            blocks.append(lax.ppermute(sent, "wall", list(enumerate(targets))))
            slots.append(tuple(w ^ targets.index(w) for w in range(count)))
        return blocks, tuple(slots)
    stack = block[None]
    for step in range(count.bit_length() - 1):
        stack = jnp.concatenate([stack, exchange(stack, "wall", 1 << step)])
    return [stack], ((0,) * count,)


def slot_here(slots):
    me = lax.axis_index("wall")
    if len(set(slots)) == 1:
        return slots[0]
    return sum(jnp.where(me == w, slot, 0) for w, slot in enumerate(slots))


VMEM = pl.BlockSpec(memory_space=pltpu.VMEM)


def call(kernel, outs, scratch, *args, aliases=None, limit=32 * 1024 * 1024):
    return pl.pallas_call(
        kernel,
        out_shape=[jax.ShapeDtypeStruct(shape, jnp.float32) for shape in outs],
        in_specs=[VMEM] * len(args),
        out_specs=[VMEM] * len(outs),
        scratch_shapes=[pltpu.VMEM(shape, jnp.float32) for shape in scratch],
        input_output_aliases=aliases or {},
        compiler_params=pltpu.CompilerParams(vmem_limit_bytes=limit),
    )(*args)


def join_kernel(state_ref, courant_ref, block_ref, sems):
    copies = [pltpu.make_async_copy(courant_ref, block_ref.at[COURANT], sems.at[PIECES])]
    for i in range(PIECES):
        piece = pl.ds(i * (COMPS // PIECES), COMPS // PIECES)
        copies.append(pltpu.make_async_copy(state_ref.at[piece], block_ref.at[piece], sems.at[i]))
    for copy in copies:
        copy.start()
    for copy in copies:
        copy.wait()


def local(state, courant, cross_sections, band_fractions, absorb_index, band_index):
    comps, stations, rows, cols = state.shape
    parts = lax.axis_size("wall")
    count = parts * rows
    ring = lax.axis_size("azim")
    tile = (rows, cols)
    block = pl.pallas_call(
        join_kernel,
        out_shape=pltpu.VMEM((TILES,) + tile, jnp.float32),
        in_specs=[pl.BlockSpec(memory_space=pl.ANY)] * 2,
        out_specs=VMEM,
        scratch_shapes=[pltpu.SemaphoreType.DMA((PIECES + 1,))],
        compiler_params=pltpu.CompilerParams(vmem_limit_bytes=60 * 1024 * 1024),
    )(state.reshape(comps, rows, cols), courant.reshape(tile))
    cross, share = band_tables(absorb_index, band_index, cross_sections, band_fractions, 1.0 / count, cols)
    blocks, ids = gather_lines(block)
    deep = (count, BANDS, cols)
    flat = (count, BANDS // 2, cols)
    whole = (parts,) + tile
    message = (1 + pl.cdiv(parts - 1, SHARE),) + tile
    ends = (parts, 2, BANDS, cols)
    both = (2,) + deep
    state_of = [ends, deep, both, message, message]
    held = []
    for arrival, (received, slot) in enumerate(zip(blocks, ids)):
        held = call(
            functools.partial(arrive_kernel, arrival, slot), state_of, [], received, cross, share, *held,
            aliases={3 + j: j for j in range(len(held))},
        )
    scratch = [flat, flat, (count + 2 * rows, cols), whole]
    my_outer, my_inner, heating, wall = call(
        first_kernel, [message, message, whole, (1, cols)], scratch, *held, aliases={3: 0, 4: 1},
    )
    inner = lax.ppermute(my_inner, "azim", [(i, i ^ 1) for i in range(ring)])
    outer = lax.ppermute(my_outer, "azim", [(i, (i + 1) % ring if i % 2 else (i - 1) % ring) for i in range(ring)])
    middle, packed = call(
        functools.partial(center_kernel, ids), [(parts, comps) + tile, (2,) + message], [], *blocks, heating,
    )
    middle, edge = call(
        border_kernel, [(parts, comps) + tile, (comps,) + tile], [(2,) + message],
        middle, packed, my_outer, my_inner, outer, inner, aliases={0: 0},
    )
    new_state, wall = call(
        functools.partial(last_kernel, ids), [(comps,) + tile, (1, cols)], [ends, deep, both] + scratch,
        blocks[0], middle, edge, wall, cross, share,
    )
    return new_state.reshape(state.shape), wall


def solution(mesh):
    return jax.shard_map(
        local,
        mesh=mesh,
        in_specs=(P(None, "case", "wall", "azim"), P("case", "wall", "azim"), P(), P(), P(), P()),
        out_specs=(P(None, "case", "wall", "azim"), P("case", "azim")),
        check_vma=False,
    )
```
